32 devices in a mesh: band: 2 (over y), space: 16 (over z, x, core).
Axes of the slice: x: 2, y: 2, z: 4, core: 2. Of those that a mesh axis runs over, the one named last changes fastest.
Arguments:
- snapshots: float32 [1152, 8, 8192], P(None, 'band', 'space'), may hold values from -6 to 6
- quad_weights: float32 [8, 8192], P('band', 'space'), may hold values from 0.2 to 9, as said below
- freq_bins: int32 [16], replicated, may hold values from 1 to 127, as said below
- block_starts: int32 [8], replicated, may hold values from 0 to 896, as said below
Outputs:
- factor: float32 [16, 2, 8, 8], P('band')
- modes: float32 [16, 2, 8, 8, 8192], P('band', None, None, None, 'space')
The draws below stay inside these ranges and needn't reach their ends.
Inputs may be any that keep to these rules, and one draw needn't show every extreme that they name: `freq_bins`: distinct and increasing; the first is 1 and the last is 127. `block_starts`: Increasing; the first is 0 and the last is 896; consecutive starts differ by 64 to 192. `quad_weights`: Positive.
All inputs are finite; a program needn't handle non-finite values.
Results may differ from the reference program's by a relative error of at most 0.000075.
Values sent between devices are 32-bit elements; how exact they have to be, the bound alone decides.
No kernel may reach another device: no remote copies, remote signals or barrier semaphores. Data moves between devices by JAX's collectives and lax.ppermute only.
A program may use at most 64 MiB of HBM per device.

```python
import math
import jax
import jax.numpy as jnp
from jax import lax

BLOCK = 256
NBLK = 8
NFREQ = 16
SLABS = 8
TIMES = 1152
SLAB = 8192
NSPACE = 65536


def draw_freq_bins(key, part):
    inner = jax.random.permutation(key, BLOCK // 2 - 3)[:NFREQ - 2] + 2
    ends = jnp.array([1, BLOCK // 2 - 1], dtype=jnp.int32)
    return jnp.sort(jnp.concatenate([ends, inner.astype(jnp.int32)])).astype(jnp.int32)


def draw_block_starts(key, part):
    jitter = jax.random.randint(key, (NBLK - 2,), -(BLOCK // 8), BLOCK // 8 + 1)
    middle = jnp.arange(1, NBLK - 1).astype(jnp.int32) * (BLOCK // 2) + jitter.astype(jnp.int32)
    first = jnp.zeros((1,), jnp.int32)
    last = jnp.full((1,), (NBLK - 1) * (BLOCK // 2), jnp.int32)
    return jnp.concatenate([first, middle, last]).astype(jnp.int32)


def draw_quad_weights(key, part):
    ramp = jnp.arange(SLAB).astype(jnp.float32) / SLAB
    spread = jax.random.uniform(key, (SLABS, SLAB), jnp.float32, jnp.log(0.3), jnp.log(3.0))
    return jnp.exp(jnp.log(3.0) * ramp)[None, :] * jnp.exp(spread)


def level_of(key, shape, pieces, smallest, high):
    factor_of = 1.0
    for axis_at, parts in pieces:
        heights = jax.random.uniform(jax.random.fold_in(jax.random.fold_in(key, 6), axis_at), (parts,), jnp.float32, smallest / len(pieces), high / len(pieces))
        factor_of = factor_of * jnp.repeat(jnp.exp(heights), shape[axis_at] // parts).reshape((-1,) + (1,) * (len(shape) - 1 - axis_at))
    return factor_of


def bell_draw(rng, shape, deviation, limit, split=(), kind=jnp.bfloat16):
    entries = jax.random.normal(rng, shape, jnp.float32) * deviation
    if len(split) > 0:
        entries = level_of(rng, shape, split, -0.22, 0.18) * entries
    return jnp.clip(entries, min=-limit, max=limit).astype(kind)


def setup_inputs(seed: int = 0) -> dict:
    keys = jax.random.split(jax.random.key(seed), 5)
    snapshots = bell_draw(keys[0], (TIMES, SLABS, SLAB), 1.0, 6.0, ((1, 2), (2, 16)), jnp.float32)
    quad_weights = draw_quad_weights(jax.random.fold_in(keys[4], 71), 0)
    freq_bins = draw_freq_bins(jax.random.fold_in(keys[4], 71), 0)
    block_starts = draw_block_starts(jax.random.fold_in(keys[4], 71), 0)
    return {"snapshots": snapshots, "quad_weights": quad_weights, "freq_bins": freq_bins, "block_starts": block_starts}


def spectral_table(freq_bins, block_starts, total_times):
    moments = jnp.arange(total_times).astype(jnp.int32)
    offset = moments[None, :] - block_starts.astype(jnp.int32)[:, None]
    inside = (offset >= 0) & (offset < BLOCK)
    position = offset.astype(jnp.float32)
    taper = 0.5 - 0.5 * jnp.cos(2.0 * math.pi * position / BLOCK)
    turns = jnp.mod(freq_bins.astype(jnp.int32)[:, None, None] * offset[None, :, :], BLOCK).astype(jnp.float32)
    phase = 2.0 * math.pi * turns / BLOCK
    scaled = jnp.where(inside, taper, 0.0)[None] / math.sqrt(0.375 * BLOCK)
    table = jnp.stack([scaled * jnp.cos(phase), -scaled * jnp.sin(phase)], axis=1)
    return table.reshape(-1, total_times)

def spectra(snap_rows, weights, table):
    fluct = snap_rows - lax.optimization_barrier(jnp.mean(snap_rows, axis=0, keepdims=True))
    coeffs = jnp.dot(table, fluct, precision=lax.Precision.HIGHEST, preferred_element_type=jnp.float32)
    return coeffs * jnp.sqrt(weights)[None, :]

def gram_split(moment):
    half = moment.shape[-1] // 2
    real_part = moment[:, :half, :half] + moment[:, half:, half:]
    imag_part = moment[:, :half, half:] - moment[:, half:, :half]
    return (real_part, imag_part)

def factor_pair(gram_real, gram_imag):
    order = gram_real.shape[-1]
    columns = jnp.arange(order)
    rows_real = []
    rows_imag = []
    for pivot_row in range(order):
        left_real = gram_real[:, pivot_row, :]
        left_imag = gram_imag[:, pivot_row, :]
        for earlier in range(pivot_row):
            coef_real = rows_real[earlier][:, pivot_row:pivot_row + 1]
            coef_imag = rows_imag[earlier][:, pivot_row:pivot_row + 1]
            left_real = left_real - (coef_real * rows_real[earlier] + coef_imag * rows_imag[earlier])
            left_imag = left_imag - (coef_real * rows_imag[earlier] - coef_imag * rows_real[earlier])
        pivot = jnp.sqrt(left_real[:, pivot_row:pivot_row + 1])
        rows_real.append(jnp.where(columns >= pivot_row, left_real / pivot, 0.0))
        rows_imag.append(jnp.where(columns > pivot_row, left_imag / pivot, 0.0))
    return (jnp.stack(rows_real, 1), jnp.stack(rows_imag, 1))

def invert_pair(fac_real, fac_imag):
    order = fac_real.shape[-1]
    identity = jnp.eye(order, dtype=fac_real.dtype)
    inv_real = [None] * order
    inv_imag = [None] * order
    for target in reversed(range(order)):
        acc_real = jnp.broadcast_to(identity[target], fac_real[:, 0, :].shape)
        acc_imag = jnp.zeros_like(acc_real)
        for later in range(target + 1, order):
            coef_real = fac_real[:, target, later:later + 1]
            coef_imag = fac_imag[:, target, later:later + 1]
            acc_real = acc_real - (coef_real * inv_real[later] - coef_imag * inv_imag[later])
            acc_imag = acc_imag - (coef_real * inv_imag[later] + coef_imag * inv_real[later])
        diagonal = fac_real[:, target, target:target + 1]
        inv_real[target] = acc_real / diagonal
        inv_imag[target] = acc_imag / diagonal
    return (jnp.stack(inv_real, 1), jnp.stack(inv_imag, 1))

def make_kernel(inv_real, inv_imag):
    upper = jnp.stack([inv_real, inv_imag], 2)
    lower = jnp.stack([-inv_imag, inv_real], 2)
    return jnp.stack([upper, lower], 1)

def reference(snapshots, quad_weights, freq_bins, block_starts):
    table = spectral_table(freq_bins, block_starts, TIMES)

    def per_slab(index):
        snap_rows = lax.dynamic_index_in_dim(snapshots, index, 1, False)
        weights = lax.dynamic_index_in_dim(quad_weights, index, 0, False)
        return spectra(snap_rows, weights, table).reshape(NFREQ, 2, NBLK, SLAB)
    coeffs = lax.map(per_slab, jnp.arange(SLABS).astype(jnp.int32))
    vectors = coeffs.reshape(SLABS, NFREQ, 2 * NBLK, SLAB)
    moment = jnp.einsum('lfas,lfbs->fab', vectors, vectors, precision=lax.Precision.HIGHEST) / NSPACE
    fac_real, fac_imag = factor_pair(*gram_split(moment))
    inv_real, inv_imag = invert_pair(fac_real, fac_imag)
    kernel = make_kernel(inv_real, inv_imag)
    modes = jnp.einsum('fpacb,lfpas->fcbls', kernel, coeffs, precision=lax.Precision.HIGHEST)
    return (jnp.stack([fac_real, fac_imag], 1), modes)
```

```python
import math

import jax
import jax.numpy as jnp
from jax import lax
from jax.experimental import pallas as pl
from jax.experimental.pallas import tpu as pltpu
from jax.sharding import PartitionSpec as P

BLOCK = 256
NBLK = 8
NFREQ = 16
SLABS = 8
GAP_LOW = 64
GAP_HIGH = 192
LANES = 128
ROWS = 8
VMEM_BYTES = 48 * 1024 * 1024
PAIRS = [(a, b) for a in range(NBLK) for b in range(a, NBLK)]
ENTRIES = [(0, a, b) for a, b in PAIRS] + [(1, a, b) for a, b in PAIRS if a < b]


def from_partner(block, axis, apart):
    count = lax.axis_size(axis)
    route = []
    for low in range(count):
        high = low | 1 << apart
        if high != low and high < count:
            route += [(low, high), (high, low)]
    return lax.ppermute(block, axis, route)


def spectral_table(freq_bins, block_starts, total_times):
    moments = jnp.arange(total_times)
    offset = moments[None, :] - block_starts[:, None]
    inside = (offset >= 0) & (offset < BLOCK)
    position = offset.astype(jnp.float32)
    taper = 0.5 - 0.5 * jnp.cos(2.0 * math.pi * position / BLOCK)
    turns = jnp.mod(freq_bins[:, None, None] * offset[None, :, :], BLOCK).astype(jnp.float32)
    phase = 2.0 * math.pi * turns / BLOCK
    scaled = jnp.where(inside, taper, 0.0)[None] / math.sqrt(0.375 * BLOCK)
    table = jnp.stack([scaled * jnp.cos(phase), -scaled * jnp.sin(phase)], axis=1)
    return table.reshape(-1, total_times)


def spectra(snap_rows, weights, table):
    fluct = snap_rows - jnp.mean(snap_rows, axis=0, keepdims=True)
    coeffs = jnp.dot(
        table, fluct, precision=lax.Precision.HIGHEST, preferred_element_type=jnp.float32
    )
    return coeffs * jnp.sqrt(weights)[None, :]


def gram_local(coeffs, count):
    vectors = coeffs.reshape(coeffs.shape[0], 2 * coeffs.shape[2], -1)
    return jnp.einsum("fas,fbs->fab", vectors, vectors, precision=lax.Precision.HIGHEST) / count


def gram_split(moment):
    half = moment.shape[-1] // 2
    real_part = moment[:, :half, :half] + moment[:, half:, half:]
    imag_part = moment[:, :half, half:] - moment[:, half:, :half]
    return (real_part, imag_part)


def factor_pair(gram_real, gram_imag):
    order = gram_real.shape[-1]
    columns = jnp.arange(order)
    rows_real = []
    rows_imag = []
    for pivot_row in range(order):
        left_real = gram_real[:, pivot_row, :]
        left_imag = gram_imag[:, pivot_row, :]
        for earlier in range(pivot_row):
            coef_real = rows_real[earlier][:, pivot_row : pivot_row + 1]
            coef_imag = rows_imag[earlier][:, pivot_row : pivot_row + 1]
            left_real = left_real - (
                coef_real * rows_real[earlier] + coef_imag * rows_imag[earlier]
            )
            left_imag = left_imag - (
                coef_real * rows_imag[earlier] - coef_imag * rows_real[earlier]
            )
        pivot = jnp.sqrt(left_real[:, pivot_row : pivot_row + 1])
        rows_real.append(jnp.where(columns >= pivot_row, left_real / pivot, 0.0))
        rows_imag.append(jnp.where(columns > pivot_row, left_imag / pivot, 0.0))
    return (jnp.stack(rows_real, 1), jnp.stack(rows_imag, 1))


def invert_pair(fac_real, fac_imag):
    order = fac_real.shape[-1]
    identity = jnp.eye(order, dtype=fac_real.dtype)
    inv_real = [None] * order
    inv_imag = [None] * order
    for target in reversed(range(order)):
        acc_real = jnp.broadcast_to(identity[target], fac_real[:, 0, :].shape)
        acc_imag = jnp.zeros_like(acc_real)
        for later in range(target + 1, order):
            coef_real = fac_real[:, target, later : later + 1]
            coef_imag = fac_imag[:, target, later : later + 1]
            acc_real = acc_real - (coef_real * inv_real[later] - coef_imag * inv_imag[later])
            acc_imag = acc_imag - (coef_real * inv_imag[later] + coef_imag * inv_real[later])
        diagonal = fac_real[:, target, target : target + 1]
        inv_real[target] = acc_real / diagonal
        inv_imag[target] = acc_imag / diagonal
    return (jnp.stack(inv_real, 1), jnp.stack(inv_imag, 1))


def project(coeffs, inv_real, inv_imag):
    upper = jnp.stack([inv_real, inv_imag], 2)
    lower = jnp.stack([-inv_imag, inv_real], 2)
    kernel = jnp.stack([upper, lower], 1)
    flat = coeffs.reshape(coeffs.shape[0], 2, coeffs.shape[2], -1)
    result = jnp.einsum("fpacb,fpas->fcbs", kernel, flat, precision=lax.Precision.HIGHEST)
    return result.reshape(coeffs.shape)


def any_bands(snapshots, quad_weights, freq_bins, block_starts):
    total_times, local_slabs, slab_cells = snapshots.shape
    table = spectral_table(freq_bins, block_starts, total_times)
    coeffs = spectra(snapshots.reshape(total_times, -1), quad_weights.reshape(-1), table)
    coeffs = coeffs.reshape(NFREQ, 2, NBLK, local_slabs, slab_cells)
    count = SLABS * slab_cells * lax.axis_size("space")
    grouped = lax.all_to_all(coeffs, "band", split_axis=0, concat_axis=3, tiled=True)
    moment = gram_local(grouped, count)
    for level in range(lax.axis_size("space").bit_length() - 1):
        moment = moment + from_partner(moment, "space", level)
    fac_real, fac_imag = factor_pair(*gram_split(moment))
    modes = project(grouped, *invert_pair(fac_real, fac_imag))
    factor = jnp.stack([fac_real, fac_imag], 1)
    return (factor, modes)


def reach(total_times):
    last = total_times - BLOCK
    spans = []
    for j in range(NBLK):
        low = max(GAP_LOW * j, last - GAP_HIGH * (NBLK - 1 - j))
        high = min(GAP_HIGH * j, last - GAP_LOW * (NBLK - 1 - j))
        spans.append((low, high + BLOCK))
    return spans


def fill_table(freq_ref, start_ref, high_ref, low_ref):
    band = lax.axis_index("band")
    wide = BLOCK + LANES
    row = lax.broadcasted_iota(jnp.int32, (NFREQ, wide), 0)
    spot = lax.broadcasted_iota(jnp.int32, (NFREQ, wide), 1)
    bins = jnp.zeros((NFREQ, wide), jnp.int32)
    half = NFREQ // 2
    for r in range(NFREQ):
        owner = 1 - band if r < half else band
        bins = jnp.where(row == r, freq_ref[owner * half + r % half], bins)
    step = 2.0 * math.pi / BLOCK
    phase = ((bins * spot) & (BLOCK - 1)).astype(jnp.float32) * step
    taper = 0.5 - 0.5 * jnp.cos(spot.astype(jnp.float32) * step)
    scaled = jnp.where(spot < BLOCK, taper, 0.0) * (1.0 / math.sqrt(0.375 * BLOCK))
    parts = (scaled * jnp.cos(phase), -scaled * jnp.sin(phase))
    high_ref[...] = jnp.zeros_like(high_ref)
    low_ref[...] = jnp.zeros_like(low_ref)
    for j in range(NBLK):
        start = start_ref[j]
        shift = start % LANES
        place = pl.ds(pl.multiple_of(start - shift, LANES), wide)
        for p in range(2):
            moved = pltpu.roll(parts[p], shift, 1)
            high = moved.astype(jnp.bfloat16)
            low = (moved - high.astype(jnp.float32)).astype(jnp.bfloat16)
            rows = pl.ds((2 * j + p) * NFREQ, NFREQ)
            high_ref[rows, place] = high
            low_ref[rows, place] = low


def coeff_chunk(flow_ref, weight, high_ref, low_ref, fhigh_ref, flow_low_ref, acc_ref, slabs):
    total = flow_ref.shape[0] // slabs
    for l in range(slabs):
        values = flow_ref[pl.ds(l, total, stride=slabs), :]
        fluct = values - jnp.sum(values, axis=0, keepdims=True) * (1.0 / total)
        high = fluct.astype(jnp.bfloat16)
        fhigh_ref[:, l * LANES : (l + 1) * LANES] = high
        flow_low_ref[:, l * LANES : (l + 1) * LANES] = (fluct - high.astype(jnp.float32)).astype(
            jnp.bfloat16
        )
    per_block = 2 * NFREQ
    spans = reach(total)
    started = [False] * NBLK
    for t0 in range(0, total, BLOCK):
        t1 = min(t0 + BLOCK, total)
        hit = [j for j in range(NBLK) if spans[j][0] < t1 and spans[j][1] > t0]
        j0, j1 = min(hit), max(hit) + 1
        rows = slice(j0 * per_block, j1 * per_block)
        xh, xl = fhigh_ref[t0:t1, :], flow_low_ref[t0:t1, :]
        th, tl = high_ref[rows, t0:t1], low_ref[rows, t0:t1]
        part = jnp.dot(th, xl, preferred_element_type=jnp.float32)
        part += jnp.dot(tl, xh, preferred_element_type=jnp.float32)
        part += jnp.dot(th, xh, preferred_element_type=jnp.float32)
        for j in range(j0, j1):
            own = slice(j * per_block, (j + 1) * per_block)
            piece = part[(j - j0) * per_block : (j - j0 + 1) * per_block]
            acc_ref[own, :] = acc_ref[own, :] + piece if started[j] else piece
            started[j] = True
    root = jnp.concatenate([jnp.sqrt(weight[l : l + 1, :]) for l in range(slabs)], axis=1)
    return root


def store_chunk(acc_ref, root, send_ref, own_ref, at):
    cols = root.shape[1]
    for jp in range(2 * NBLK):
        piece = acc_ref[jp * 2 * ROWS : (jp + 1) * 2 * ROWS, :] * root
        send_ref[jp, :, at : at + cols] = piece[:ROWS]
        own_ref[jp, :, at : at + cols] = piece[ROWS:]


def spectra_kernel(slabs, first, count, freq_ref, start_ref, snap_ref, weight_ref, *rest):
    send_ref, own_ref, held, high_ref, low_ref, fh_ref, fl_ref, acc_ref, sems = rest
    copies = []
    for i in range(count):
        source = snap_ref.at[:, :, pl.ds((first + i) * LANES, LANES)]
        copies.append(pltpu.make_async_copy(source, held.at[i], sems.at[i]))
        copies[-1].start()
    fill_table(freq_ref, start_ref, high_ref, low_ref)
    total = snap_ref.shape[0]
    for i in range(count):
        copies[i].wait()
        flat = held.at[i].reshape(total * slabs, LANES)
        weight = weight_ref[:, (first + i) * LANES : (first + i + 1) * LANES]
        root = coeff_chunk(flat, weight, high_ref, low_ref, fh_ref, fl_ref, acc_ref, slabs)
        store_chunk(acc_ref, root, send_ref, own_ref, i * slabs * LANES)


def spectra_call(snapshots, weights, freq_bins, block_starts, first, count):
    total, slabs, _ = snapshots.shape
    cols = slabs * LANES
    shape = jax.ShapeDtypeStruct((2 * NBLK, ROWS, count * cols), jnp.float32)
    wide = -(-total // LANES) * LANES + LANES
    return pl.pallas_call(
        lambda *refs: spectra_kernel(slabs, first, count, *refs),
        out_shape=(shape, shape),
        in_specs=[
            pl.BlockSpec(memory_space=pltpu.SMEM),
            pl.BlockSpec(memory_space=pltpu.SMEM),
            pl.BlockSpec(memory_space=pl.ANY),
            pl.BlockSpec(memory_space=pltpu.VMEM),
        ],
        out_specs=(pl.BlockSpec(memory_space=pltpu.VMEM),) * 2,
        scratch_shapes=[
            pltpu.VMEM((count, total, slabs, LANES), jnp.float32),
            pltpu.VMEM((2 * NBLK * NFREQ, wide), jnp.bfloat16),
            pltpu.VMEM((2 * NBLK * NFREQ, wide), jnp.bfloat16),
            pltpu.VMEM((total, cols), jnp.bfloat16),
            pltpu.VMEM((total, cols), jnp.bfloat16),
            pltpu.VMEM((2 * NBLK * NFREQ, cols), jnp.float32),
            pltpu.SemaphoreType.DMA((count,)),
        ],
        compiler_params=pltpu.CompilerParams(vmem_limit_bytes=VMEM_BYTES),
        name="spectra",
    )(freq_bins, block_starts, snapshots, weights)


def lane_places(count):
    bits = LANES.bit_length() - 1
    used = count.bit_length() - 1
    lanes = []
    for e in range(count):
        lane = 0
        for level in range(used):
            if e >> (used - 1 - level) & 1:
                lane |= 1 << level
        lanes.append(lane)
    return lanes


def fold_lanes(terms):
    lane = lax.broadcasted_iota(jnp.int32, (ROWS, LANES), 1)
    apart = 1
    while len(terms) > 1:
        half = len(terms) // 2
        kept = (lane & apart) == 0
        merged = []
        for i in range(half):
            first, second = terms[i], terms[i + half]
            stay = jnp.where(kept, first, second)
            go = jnp.where(kept, second, first)
            fold = jnp.where(
                kept, pltpu.roll(go, LANES - apart, 1), pltpu.roll(go, apart, 1)
            )
            merged.append(stay + fold)
        terms = merged
        apart *= 2
    total = terms[0]
    while apart < LANES:
        total = total + pltpu.roll(total, apart, 1)
        apart *= 2
    return total


def gram_kernel(*refs):
    blocks, outs = refs[:-2], refs[-2:]
    pairs = len(blocks) // 2
    for side in range(2):
        sums = {}
        for a in range(NBLK):
            row = [(0, a, b) for b in range(a, NBLK)] + [(1, a, b) for b in range(a + 1, NBLK)]
            carry = tuple(jnp.zeros((ROWS, LANES), jnp.float32) for _ in row)
            for i in range(pairs):
                ref = blocks[2 * i + side]

                def body(k, carry, ref=ref, a=a, row=row):
                    cols = pl.ds(pl.multiple_of(k * LANES, LANES), LANES)
                    re = {b: ref[2 * b, :, cols] for b in range(a, NBLK)}
                    im = {b: ref[2 * b + 1, :, cols] for b in range(a, NBLK)}
                    out = []
                    for (kind, _, b), total in zip(row, carry):
                        if kind == 0:
                            out.append(total + (re[a] * re[b] + im[a] * im[b]))
                        else:
                            out.append(total + (re[a] * im[b] - im[a] * re[b]))
                    return tuple(out)

                carry = lax.fori_loop(0, ref.shape[2] // LANES, body, carry, unroll=4)
            for key, total in zip(row, carry):
                sums[key] = total
        outs[side][...] = fold_lanes([sums[key] for key in ENTRIES])


def gram_call(*blocks):
    shape = jax.ShapeDtypeStruct((ROWS, LANES), jnp.float32)
    return pl.pallas_call(
        gram_kernel,
        out_shape=(shape, shape),
        in_specs=[pl.BlockSpec(memory_space=pltpu.VMEM)] * len(blocks),
        out_specs=(pl.BlockSpec(memory_space=pltpu.VMEM),) * 2,
        compiler_params=pltpu.CompilerParams(vmem_limit_bytes=VMEM_BYTES),
        name="gram",
    )(*blocks)


def factor_kernel(count, sum_ref, inv_ref, fac_ref):
    total = sum_ref[...] * (1.0 / count)
    wide = lambda v: jnp.broadcast_to(v, (ROWS, LANES))
    gram = {
        key: wide(total[:, lane : lane + 1]) for key, lane in zip(ENTRIES, lane_places(len(ENTRIES)))
    }
    fac, recip = {}, []
    for r in range(NBLK):
        for c in range(r, NBLK):
            real = gram[0, r, c]
            imag = gram[1, r, c] if c > r else None
            for e in range(r):
                ar, ai = fac[0, e, r], fac[1, e, r]
                br, bi = fac[0, e, c], fac[1, e, c]
                real = real - (ar * br + ai * bi)
                if c > r:
                    imag = imag - (ar * bi - ai * br)
            if c == r:
                pivot = jnp.sqrt(real)
                fac[0, r, r] = pivot
                recip.append(1.0 / pivot)
            else:
                fac[0, r, c] = real * recip[r]
                fac[1, r, c] = imag * recip[r]
    inv = {}
    for b in range(NBLK):
        inv[0, b, b] = recip[b]
        for a in reversed(range(b)):
            real = imag = jnp.zeros((ROWS, LANES), jnp.float32)
            for k in range(a + 1, b + 1):
                cr, ci = fac[0, a, k], fac[1, a, k]
                real = real - cr * inv[0, k, b]
                imag = imag - ci * inv[0, k, b]
                if k < b:
                    real = real + ci * inv[1, k, b]
                    imag = imag - cr * inv[1, k, b]
            inv[0, a, b] = real * recip[a]
            inv[1, a, b] = imag * recip[a]
    for e, key in enumerate(ENTRIES):
        inv_ref[e] = inv[key]
    lane = lax.broadcasted_iota(jnp.int32, (ROWS, LANES), 1)
    for p in range(2):
        for a in range(NBLK):
            line = jnp.zeros((ROWS, LANES), jnp.float32)
            for b in range(a + p, NBLK):
                line = jnp.where(lane == b, fac[p, a, b], line)
            fac_ref[pl.ds(p * NBLK + a, ROWS, stride=2 * NBLK), :] = line


def factor_call(total, count):
    return pl.pallas_call(
        lambda *refs: factor_kernel(count, *refs),
        out_shape=(
            jax.ShapeDtypeStruct((len(ENTRIES), ROWS, LANES), jnp.float32),
            jax.ShapeDtypeStruct((ROWS * 2 * NBLK, LANES), jnp.float32),
        ),
        in_specs=[pl.BlockSpec(memory_space=pltpu.VMEM)],
        out_specs=(pl.BlockSpec(memory_space=pltpu.VMEM),) * 2,
        compiler_params=pltpu.CompilerParams(vmem_limit_bytes=VMEM_BYTES),
        name="factor",
    )(total)


def project_kernel(slabs, inv_ref, own_ref, far_ref, *rest):
    out_ref = rest[-1]
    band = lax.axis_index("band")
    per = 2 * NBLK * 2 * slabs
    flat = out_ref.reshape(ROWS * per, LANES)
    for side, ref in enumerate((own_ref, far_ref)):
        base = (band if side == 0 else 1 - band) * slabs

        def body(l, _, ref=ref, base=base):
            cols = pl.ds(pl.multiple_of(l * LANES, LANES), LANES)
            re = [ref[2 * a, :, cols] for a in range(NBLK)]
            im = [ref[2 * a + 1, :, cols] for a in range(NBLK)]
            for b in range(NBLK):
                diagonal = inv_ref[ENTRIES.index((0, b, b))]
                real, imag = re[b] * diagonal, im[b] * diagonal
                for a in range(b):
                    cr = inv_ref[ENTRIES.index((0, a, b))]
                    ci = inv_ref[ENTRIES.index((1, a, b))]
                    real = real + (re[a] * cr - im[a] * ci)
                    imag = imag + (re[a] * ci + im[a] * cr)
                for p, value in enumerate((real, imag)):
                    line = (p * NBLK + b) * 2 * slabs + base + l
                    flat[pl.ds(line, ROWS, stride=per), :] = value
            return 0

        lax.fori_loop(0, slabs, body, 0, unroll=2)


def project_call(inv, own, far, modes, at, slabs, chunks):
    count = own.shape[2] // (slabs * LANES)
    block = (ROWS, 2 * NBLK, None, 2 * slabs, LANES)
    given = [] if modes is None else [modes]
    cols = slabs * LANES
    spec = pl.BlockSpec((2 * NBLK, ROWS, cols), lambda i: (0, 0, i))
    return pl.pallas_call(
        lambda *refs: project_kernel(slabs, *refs),
        grid=(count,),
        out_shape=jax.ShapeDtypeStruct((ROWS, 2 * NBLK, chunks, 2 * slabs, LANES), jnp.float32),
        in_specs=[pl.BlockSpec(inv.shape, lambda i: (0, 0, 0)), spec, spec]
        + [pl.BlockSpec(memory_space=pl.ANY)] * len(given),
        out_specs=pl.BlockSpec(block, lambda i: (0, 0, at + i, 0, 0)),
        input_output_aliases={3: 0} if given else {},
        compiler_params=pltpu.CompilerParams(vmem_limit_bytes=VMEM_BYTES),
        name="project",
    )(inv, own, far, *given)


def swap_bands(block):
    return lax.ppermute(block, "band", [(0, 1), (1, 0)])


def two_bands(snapshots, quad_weights, freq_bins, block_starts):
    slabs, cells = snapshots.shape[1:]
    chunks = cells // LANES
    count = 2 * slabs * cells * lax.axis_size("space")
    given = (snapshots, quad_weights, freq_bins, block_starts)
    send_a, own_a = spectra_call(*given, 0, 1)
    far_a = swap_bands(send_a)
    send_b, own_b = spectra_call(*given, 1, chunks - 1)
    gram_send, gram_own = gram_call(send_a, own_a, send_b, own_b)
    total = gram_own + swap_bands(gram_send)
    far_b = swap_bands(send_b)
    for level in range(lax.axis_size("space").bit_length() - 1):
        total = total + from_partner(total, "space", level)
    inv, fac = factor_call(total, count)
    modes = project_call(inv, own_a, far_a, None, 0, slabs, chunks)
    modes = project_call(inv, own_b, far_b, modes, 1, slabs, chunks)
    modes = modes.reshape(ROWS, 2, NBLK, chunks, 2 * slabs, LANES)
    modes = modes.transpose(0, 1, 2, 4, 3, 5).reshape(ROWS, 2, NBLK, 2 * slabs, cells)
    factor = fac[:, :NBLK].reshape(ROWS, 2, NBLK, NBLK)
    return (factor, modes)


def shards(snapshots, *others):
    fits = NFREQ == ROWS * lax.axis_size("band") == 2 * ROWS
    fits = fits and snapshots.shape[1] == SLABS // 2 and snapshots.shape[2] % LANES == 0
    fits = fits and snapshots.shape[2] > LANES and snapshots.shape[0] % LANES == 0
    return (two_bands if fits else any_bands)(snapshots, *others)


def solution(mesh):
    placed = (P(None, "band", "space"), P("band", "space"), P(), P())
    return jax.shard_map(
        shards,
        mesh=mesh,
        in_specs=placed,
        out_specs=(P("band", None, None, None), P("band", None, None, None, "space")),
        check_vma=False,
    )
```

```python
import math

import jax
import jax.numpy as jnp
from jax import lax
from jax.experimental import pallas as pl
from jax.experimental.pallas import tpu as pltpu
from jax.sharding import PartitionSpec as P

BLOCK = 256
NBLK = 8
NFREQ = 16
SLABS = 8
GAP_LOW = 64
GAP_HIGH = 192
LANES = 128
ROWS = 8
JOIN_FLOPS = 10**10
VMEM_BYTES = 48 * 1024 * 1024
PAIRS = [(a, b) for a in range(NBLK) for b in range(a, NBLK)]
ENTRIES = [(0, a, b) for a, b in PAIRS] + [(1, a, b) for a, b in PAIRS if a < b]


def from_partner(block, axis, apart):
    count = lax.axis_size(axis)
    route = []
    for low in range(count):
        high = low | 1 << apart
        if high != low and high < count:
            route += [(low, high), (high, low)]
    return lax.ppermute(block, axis, route)


def spectral_table(freq_bins, block_starts, total_times):
    moments = jnp.arange(total_times)
    offset = moments[None, :] - block_starts[:, None]
    inside = (offset >= 0) & (offset < BLOCK)
    position = offset.astype(jnp.float32)
    taper = 0.5 - 0.5 * jnp.cos(2.0 * math.pi * position / BLOCK)
    turns = jnp.mod(freq_bins[:, None, None] * offset[None, :, :], BLOCK).astype(jnp.float32)
    phase = 2.0 * math.pi * turns / BLOCK
    scaled = jnp.where(inside, taper, 0.0)[None] / math.sqrt(0.375 * BLOCK)
    table = jnp.stack([scaled * jnp.cos(phase), -scaled * jnp.sin(phase)], axis=1)
    return table.reshape(-1, total_times)


def spectra(snap_rows, weights, table):
    fluct = snap_rows - jnp.mean(snap_rows, axis=0, keepdims=True)
    coeffs = jnp.dot(
        table, fluct, precision=lax.Precision.HIGHEST, preferred_element_type=jnp.float32
    )
    return coeffs * jnp.sqrt(weights)[None, :]


def gram_local(coeffs, count):
    vectors = coeffs.reshape(coeffs.shape[0], 2 * coeffs.shape[2], -1)
    return jnp.einsum("fas,fbs->fab", vectors, vectors, precision=lax.Precision.HIGHEST) / count


def gram_split(moment):
    half = moment.shape[-1] // 2
    real_part = moment[:, :half, :half] + moment[:, half:, half:]
    imag_part = moment[:, :half, half:] - moment[:, half:, :half]
    return (real_part, imag_part)


def factor_pair(gram_real, gram_imag):
    order = gram_real.shape[-1]
    columns = jnp.arange(order)
    rows_real = []
    rows_imag = []
    for pivot_row in range(order):
        left_real = gram_real[:, pivot_row, :]
        left_imag = gram_imag[:, pivot_row, :]
        for earlier in range(pivot_row):
            coef_real = rows_real[earlier][:, pivot_row : pivot_row + 1]
            coef_imag = rows_imag[earlier][:, pivot_row : pivot_row + 1]
            left_real = left_real - (
                coef_real * rows_real[earlier] + coef_imag * rows_imag[earlier]
            )
            left_imag = left_imag - (
                coef_real * rows_imag[earlier] - coef_imag * rows_real[earlier]
            )
        pivot = jnp.sqrt(left_real[:, pivot_row : pivot_row + 1])
        rows_real.append(jnp.where(columns >= pivot_row, left_real / pivot, 0.0))
        rows_imag.append(jnp.where(columns > pivot_row, left_imag / pivot, 0.0))
    return (jnp.stack(rows_real, 1), jnp.stack(rows_imag, 1))


def invert_pair(fac_real, fac_imag):
    order = fac_real.shape[-1]
    identity = jnp.eye(order, dtype=fac_real.dtype)
    inv_real = [None] * order
    inv_imag = [None] * order
    for target in reversed(range(order)):
        acc_real = jnp.broadcast_to(identity[target], fac_real[:, 0, :].shape)
        acc_imag = jnp.zeros_like(acc_real)
        for later in range(target + 1, order):
            coef_real = fac_real[:, target, later : later + 1]
            coef_imag = fac_imag[:, target, later : later + 1]
            acc_real = acc_real - (coef_real * inv_real[later] - coef_imag * inv_imag[later])
            acc_imag = acc_imag - (coef_real * inv_imag[later] + coef_imag * inv_real[later])
        diagonal = fac_real[:, target, target : target + 1]
        inv_real[target] = acc_real / diagonal
        inv_imag[target] = acc_imag / diagonal
    return (jnp.stack(inv_real, 1), jnp.stack(inv_imag, 1))


def project(coeffs, inv_real, inv_imag):
    upper = jnp.stack([inv_real, inv_imag], 2)
    lower = jnp.stack([-inv_imag, inv_real], 2)
    kernel = jnp.stack([upper, lower], 1)
    flat = coeffs.reshape(coeffs.shape[0], 2, coeffs.shape[2], -1)
    result = jnp.einsum("fpacb,fpas->fcbs", kernel, flat, precision=lax.Precision.HIGHEST)
    return result.reshape(coeffs.shape)


def any_bands(snapshots, quad_weights, freq_bins, block_starts):
    total_times, local_slabs, slab_cells = snapshots.shape
    table = spectral_table(freq_bins, block_starts, total_times)
    coeffs = spectra(snapshots.reshape(total_times, -1), quad_weights.reshape(-1), table)
    coeffs = coeffs.reshape(NFREQ, 2, NBLK, local_slabs, slab_cells)
    count = SLABS * slab_cells * lax.axis_size("space")
    grouped = lax.all_to_all(coeffs, "band", split_axis=0, concat_axis=3, tiled=True)
    moment = gram_local(grouped, count)
    for level in range(lax.axis_size("space").bit_length() - 1):
        moment = moment + from_partner(moment, "space", level)
    fac_real, fac_imag = factor_pair(*gram_split(moment))
    modes = project(grouped, *invert_pair(fac_real, fac_imag))
    factor = jnp.stack([fac_real, fac_imag], 1)
    return (factor, modes)


def reach(total_times):
    last = total_times - BLOCK
    spans = []
    for j in range(NBLK):
        low = max(GAP_LOW * j, last - GAP_HIGH * (NBLK - 1 - j))
        high = min(GAP_HIGH * j, last - GAP_LOW * (NBLK - 1 - j))
        spans.append((low, high + BLOCK))
    return spans


def fill_table(freq_ref, start_ref, high_ref, low_ref):
    band = lax.axis_index("band")
    wide = BLOCK + LANES
    row = lax.broadcasted_iota(jnp.int32, (NFREQ, wide), 0)
    spot = lax.broadcasted_iota(jnp.int32, (NFREQ, wide), 1)
    bins = jnp.zeros((NFREQ, wide), jnp.int32)
    half = NFREQ // 2
    for r in range(NFREQ):
        owner = 1 - band if r < half else band
        bins = jnp.where(row == r, freq_ref[owner * half + r % half], bins)
    step = 2.0 * math.pi / BLOCK
    phase = ((bins * spot) & (BLOCK - 1)).astype(jnp.float32) * step
    taper = 0.5 - 0.5 * jnp.cos(spot.astype(jnp.float32) * step)
    scaled = jnp.where(spot < BLOCK, taper, 0.0) * (1.0 / math.sqrt(0.375 * BLOCK))
    parts = (scaled * jnp.cos(phase), -scaled * jnp.sin(phase))
    high_ref[...] = jnp.zeros_like(high_ref)
    low_ref[...] = jnp.zeros_like(low_ref)
    for j in range(NBLK):
        start = start_ref[j]
        shift = start % LANES
        place = pl.ds(pl.multiple_of(start - shift, LANES), wide)
        for p in range(2):
            moved = pltpu.roll(parts[p], shift, 1)
            high = moved.astype(jnp.bfloat16)
            low = (moved - high.astype(jnp.float32)).astype(jnp.bfloat16)
            rows = pl.ds((2 * j + p) * NFREQ, NFREQ)
            high_ref[rows, place] = high
            low_ref[rows, place] = low
    return [jnp.sum(part, axis=1, keepdims=True) for part in parts]


def coeff_chunk(flow_ref, arrived, high_ref, low_ref, fh_ref, fl_ref, acc_ref, slabs):
    total = flow_ref.shape[0] // slabs
    per_block = 2 * NFREQ
    spans = reach(total)
    started = [False] * NBLK
    shift, left = [None] * slabs, [0.0] * slabs
    for i, t0 in enumerate(range(0, total, BLOCK)):
        t1 = min(t0 + BLOCK, total)
        arrived(i)
        for l in range(slabs):
            values = flow_ref[pl.ds(t0 * slabs + l, t1 - t0, stride=slabs), :]
            if i == 0:
                shift[l] = jnp.sum(values, axis=0, keepdims=True) * (1.0 / (t1 - t0))
            values = values - shift[l]
            left[l] += jnp.sum(values.reshape(-1, ROWS, LANES), axis=0)
            high = values.astype(jnp.bfloat16)
            cols = slice(l * LANES, (l + 1) * LANES)
            fh_ref[t0:t1, cols] = high
            fl_ref[t0:t1, cols] = (values - high.astype(jnp.float32)).astype(jnp.bfloat16)
    for i, t0 in enumerate(range(0, total, BLOCK)):
        t1 = min(t0 + BLOCK, total)
        hit = [j for j in range(NBLK) if spans[j][0] < t1 and spans[j][1] > t0]
        j0, j1 = min(hit), max(hit) + 1
        rows = slice(j0 * per_block, j1 * per_block)
        xh, xl = fh_ref[t0:t1, :], fl_ref[t0:t1, :]
        th, tl = high_ref[rows, t0:t1], low_ref[rows, t0:t1]
        part = jnp.dot(
            jnp.concatenate([th, tl, th], axis=1),
            jnp.concatenate([xh, xh, xl], axis=0),
            preferred_element_type=jnp.float32,
        )
        for j in range(j0, j1):
            own = slice(j * per_block, (j + 1) * per_block)
            piece = part[(j - j0) * per_block : (j - j0 + 1) * per_block]
            acc_ref[own, :] = acc_ref[own, :] + piece if started[j] else piece
            started[j] = True
    left = [jnp.sum(rest, axis=0, keepdims=True) * (1.0 / total) for rest in left]
    return jnp.concatenate(left, axis=1)


def store_chunk(acc_ref, left, sums, root, send_ref, own_ref):
    for p in range(2):
        mean_part = sums[p] * left
        for j in range(NBLK):
            jp = 2 * j + p
            piece = (acc_ref[jp * NFREQ : (jp + 1) * NFREQ, :] - mean_part) * root
            send_ref[jp] = piece[:ROWS]
            own_ref[jp] = piece[ROWS:]


def spectra_kernel(slabs, first, pieces, earlier, *refs):
    freq_hbm, start_hbm, snap_ref, weight_hbm, *rest = refs
    count = sum(pieces)
    outs = len(pieces)
    sends, owns, rest = rest[:outs], rest[outs : 2 * outs], rest[2 * outs :]
    if earlier:
        gram_ref, *rest = rest
    freq_ref, start_ref, weight_ref, held = rest[:4]
    high_ref, low_ref, fh_ref, fl_ref, acc_ref, sems, small_sems = rest[4:]
    small = [
        pltpu.make_async_copy(source, target, small_sems.at[i])
        for i, (source, target) in enumerate(
            ((freq_hbm, freq_ref), (start_hbm, start_ref), (weight_hbm, weight_ref))
        )
    ]
    for copy in small:
        copy.start()
    total = snap_ref.shape[0]
    copies = []
    for i in range(count):
        copies.append([])
        step = total
        for k, t0 in enumerate(range(0, total, step)):
            times = pl.ds(t0, min(step, total - t0))
            source = snap_ref.at[times, :, pl.ds((first + i) * LANES, LANES)]
            copies[i].append(pltpu.make_async_copy(source, held.at[i, times], sems.at[i, k]))
            copies[i][k].start()
    for copy in small:
        copy.wait()
    sums = fill_table(freq_ref, start_ref, high_ref, low_ref)
    places = [(piece, at) for piece, size in enumerate(pieces) for at in range(size)]
    for i in range(count):
        flat = held.at[i].reshape(total * slabs, LANES)
        weight = weight_ref[:, (first + i) * LANES : (first + i + 1) * LANES]
        root = jnp.concatenate([jnp.sqrt(weight[l : l + 1, :]) for l in range(slabs)], axis=1)
        left = coeff_chunk(
            flat, lambda k: copies[i][k].wait() if k < len(copies[i]) else None, high_ref, low_ref, fh_ref, fl_ref, acc_ref, slabs
        )
        piece, at = places[i]
        cols = slice(at * slabs * LANES, (at + 1) * slabs * LANES)
        store_chunk(acc_ref, left, sums, root, sends[piece].at[:, :, cols], owns[piece].at[:, :, cols])
    if earlier:
        gram_ref[...] = gram_sums([*earlier, *sends])


def spectra_call(snapshots, weights, freq_bins, block_starts, first, pieces, earlier=()):
    total, slabs, _ = snapshots.shape
    cols = slabs * LANES
    count, outs, more = sum(pieces), len(pieces), len(earlier)
    shapes = [jax.ShapeDtypeStruct((2 * NBLK, ROWS, n * cols), jnp.float32) for n in pieces] * 2
    if more:
        shapes.append(jax.ShapeDtypeStruct((ROWS, LANES), jnp.float32))
    wide = -(-total // LANES) * LANES + LANES
    given = pl.pallas_call(
        lambda *refs: spectra_kernel(
            slabs, first, pieces, refs[4 : 4 + more], *refs[:4], *refs[4 + more :]
        ),
        out_shape=tuple(shapes),
        in_specs=[pl.BlockSpec(memory_space=pltpu.HBM)] * 4
        + [pl.BlockSpec(memory_space=pltpu.VMEM)] * more,
        out_specs=(pl.BlockSpec(memory_space=pltpu.VMEM),) * len(shapes),
        scratch_shapes=[
            pltpu.SMEM(freq_bins.shape, jnp.int32),
            pltpu.SMEM(block_starts.shape, jnp.int32),
            pltpu.VMEM(weights.shape, jnp.float32),
            pltpu.VMEM((count, total, slabs, LANES), jnp.float32),
            pltpu.VMEM((2 * NBLK * NFREQ, wide), jnp.bfloat16),
            pltpu.VMEM((2 * NBLK * NFREQ, wide), jnp.bfloat16),
            pltpu.VMEM((total, cols), jnp.bfloat16),
            pltpu.VMEM((total, cols), jnp.bfloat16),
            pltpu.VMEM((2 * NBLK * NFREQ, cols), jnp.float32),
            pltpu.SemaphoreType.DMA((count, -(-total // BLOCK))),
            pltpu.SemaphoreType.DMA((3,)),
        ],
        compiler_params=pltpu.CompilerParams(vmem_limit_bytes=VMEM_BYTES),
        cost_estimate=pl.CostEstimate(
            flops=6 * 2 * NBLK * NFREQ * total * count * cols,
            bytes_accessed=4 * (total + 2 * NBLK * NFREQ) * count * cols,
            transcendentals=0,
        ),
        name="spectra",
    )(freq_bins, block_starts, snapshots, weights, *earlier)
    return given[:outs], given[outs : 2 * outs], given[2 * outs :]


def lane_places(count):
    bits = LANES.bit_length() - 1
    used = count.bit_length() - 1
    lanes = []
    for e in range(count):
        lane = 0
        for level in range(used):
            if e >> (used - 1 - level) & 1:
                lane |= 1 << level
        lanes.append(lane)
    return lanes


def fold_lanes(terms):
    lane = lax.broadcasted_iota(jnp.int32, (ROWS, LANES), 1)
    apart = 1
    while len(terms) > 1:
        half = len(terms) // 2
        kept = (lane & apart) == 0
        merged = []
        for i in range(half):
            first, second = terms[i], terms[i + half]
            stay = jnp.where(kept, first, second)
            go = jnp.where(kept, second, first)
            fold = jnp.where(
                kept, pltpu.roll(go, LANES - apart, 1), pltpu.roll(go, apart, 1)
            )
            merged.append(stay + fold)
        terms = merged
        apart *= 2
    total = terms[0]
    while apart < LANES:
        total = total + pltpu.roll(total, apart, 1)
        apart *= 2
    return total


def gram_sums(blocks):
    sums = {}
    for a in range(NBLK):
        row = [(0, a, b) for b in range(a, NBLK)] + [(1, a, b) for b in range(a + 1, NBLK)]
        carry = tuple(jnp.zeros((ROWS, LANES), jnp.float32) for _ in row)
        for ref in blocks:

            def body(k, carry, ref=ref, a=a, row=row):
                cols = pl.ds(pl.multiple_of(k * LANES, LANES), LANES)
                re = {b: ref[2 * b, :, cols] for b in range(a, NBLK)}
                im = {b: ref[2 * b + 1, :, cols] for b in range(a, NBLK)}
                out = []
                for (kind, _, b), total in zip(row, carry):
                    if kind == 0:
                        out.append(total + (re[a] * re[b] + im[a] * im[b]))
                    else:
                        out.append(total + (re[a] * im[b] - im[a] * re[b]))
                return tuple(out)

            carry = lax.fori_loop(0, ref.shape[2] // LANES, body, carry, unroll=4)
        for key, total in zip(row, carry):
            sums[key] = total
    return fold_lanes([sums[key] for key in ENTRIES])


def gram_kernel(count, *refs):
    refs[-1][...] = gram_sums(refs[:count])


def gram_call(blocks, after):
    return pl.pallas_call(
        lambda *refs: gram_kernel(len(blocks), *refs),
        out_shape=jax.ShapeDtypeStruct((ROWS, LANES), jnp.float32),
        in_specs=[pl.BlockSpec(memory_space=pltpu.VMEM)] * len(blocks)
        + [pl.BlockSpec(memory_space=pl.ANY)],
        out_specs=pl.BlockSpec(memory_space=pltpu.VMEM),
        compiler_params=pltpu.CompilerParams(vmem_limit_bytes=VMEM_BYTES),
        cost_estimate=pl.CostEstimate(
            flops=sum(block.size for block in blocks) * 4 * NBLK,
            bytes_accessed=4 * sum(block.size for block in blocks),
            transcendentals=0,
        ),
        name="gram",
    )(*blocks, after)


def join_kernel(own_ref, far_ref, out_ref):
    out_ref[...] = own_ref[...] + far_ref[...]


def join_call(own, far):
    return pl.pallas_call(
        join_kernel,
        out_shape=jax.ShapeDtypeStruct(own.shape, own.dtype),
        in_specs=[pl.BlockSpec(memory_space=pltpu.VMEM)] * 2,
        out_specs=pl.BlockSpec(memory_space=pltpu.VMEM),
        compiler_params=pltpu.CompilerParams(vmem_limit_bytes=VMEM_BYTES),
        cost_estimate=pl.CostEstimate(flops=JOIN_FLOPS, bytes_accessed=0, transcendentals=0),
        name="join",
    )(own, far)


def factor_kernel(count, sum_ref, inv_ref, fac_ref):
    total = sum_ref[...] * (1.0 / count)
    wide = lambda v: jnp.broadcast_to(v, (ROWS, LANES))
    gram = {
        key: wide(total[:, lane : lane + 1]) for key, lane in zip(ENTRIES, lane_places(len(ENTRIES)))
    }
    fac, recip = {}, []
    for r in range(NBLK):
        for c in range(r, NBLK):
            real = gram[0, r, c]
            imag = gram[1, r, c] if c > r else None
            for e in range(r):
                ar, ai = fac[0, e, r], fac[1, e, r]
                br, bi = fac[0, e, c], fac[1, e, c]
                real = real - (ar * br + ai * bi)
                if c > r:
                    imag = imag - (ar * bi - ai * br)
            if c == r:
                pivot = jnp.sqrt(real)
                fac[0, r, r] = pivot
                recip.append(1.0 / pivot)
            else:
                fac[0, r, c] = real * recip[r]
                fac[1, r, c] = imag * recip[r]
    inv = {}
    for b in range(NBLK):
        inv[0, b, b] = recip[b]
        for a in reversed(range(b)):
            real = imag = jnp.zeros((ROWS, LANES), jnp.float32)
            for k in range(a + 1, b + 1):
                cr, ci = fac[0, a, k], fac[1, a, k]
                real = real - cr * inv[0, k, b]
                imag = imag - ci * inv[0, k, b]
                if k < b:
                    real = real + ci * inv[1, k, b]
                    imag = imag - cr * inv[1, k, b]
            inv[0, a, b] = real * recip[a]
            inv[1, a, b] = imag * recip[a]
    for e, key in enumerate(ENTRIES):
        inv_ref[e] = inv[key]
    lane = lax.broadcasted_iota(jnp.int32, (ROWS, LANES), 1)
    for p in range(2):
        for a in range(NBLK):
            line = jnp.zeros((ROWS, LANES), jnp.float32)
            for b in range(a + p, NBLK):
                line = jnp.where(lane == b, fac[p, a, b], line)
            fac_ref[pl.ds(p * NBLK + a, ROWS, stride=2 * NBLK), :] = line


def factor_call(total, count):
    return pl.pallas_call(
        lambda *refs: factor_kernel(count, *refs),
        out_shape=(
            jax.ShapeDtypeStruct((len(ENTRIES), ROWS, LANES), jnp.float32),
            jax.ShapeDtypeStruct((ROWS * 2 * NBLK, LANES), jnp.float32),
        ),
        in_specs=[pl.BlockSpec(memory_space=pltpu.VMEM)],
        out_specs=(pl.BlockSpec(memory_space=pltpu.VMEM),) * 2,
        compiler_params=pltpu.CompilerParams(vmem_limit_bytes=VMEM_BYTES),
        name="factor",
    )(total)


def project_chunk(slabs, inv_ref, own_ref, far_ref, first, flat):
    band = lax.axis_index("band")
    per = 2 * NBLK * 2 * slabs
    for side, ref in enumerate((own_ref, far_ref)):
        base = (band if side == 0 else 1 - band) * slabs
        for l0 in range(0, slabs, 2):
            both = range(l0, l0 + 2)
            cols = [pl.ds(pl.multiple_of(first + l * LANES, LANES), LANES) for l in both]
            re = [[ref[2 * a, :, at] for a in range(NBLK)] for at in cols]
            im = [[ref[2 * a + 1, :, at] for a in range(NBLK)] for at in cols]
            for b in range(NBLK):
                diagonal = inv_ref[ENTRIES.index((0, b, b))]
                real = [re[i][b] * diagonal for i in range(2)]
                imag = [im[i][b] * diagonal for i in range(2)]
                for a in range(b):
                    cr = inv_ref[ENTRIES.index((0, a, b))]
                    ci = inv_ref[ENTRIES.index((1, a, b))]
                    for i in range(2):
                        real[i] = real[i] + (re[i][a] * cr - im[i][a] * ci)
                        imag[i] = imag[i] + (re[i][a] * ci + im[i][a] * cr)
                for i in range(2):
                    for p, value in enumerate((real[i], imag[i])):
                        line = (p * NBLK + b) * 2 * slabs + base + l0 + i
                        flat[pl.ds(line, ROWS, stride=per), :] = value


def project_kernel(slabs, at, inv_ref, own_ref, far_ref, *rest):
    out_ref, held, sems = rest[-3:]
    count = held.shape[0]
    per = 2 * NBLK * 2 * slabs

    def copy_of(i):
        return pltpu.make_async_copy(held.at[i], out_ref.at[:, :, at + i], sems.at[i])

    def body(i, _):
        flat = held.at[i].reshape(ROWS * per, LANES)
        project_chunk(slabs, inv_ref, own_ref, far_ref, i * slabs * LANES, flat)
        copy_of(i).start()
        return 0

    lax.fori_loop(0, count, body, 0)
    for i in range(count):
        copy_of(i).wait()


def project_call(inv, own, far, modes, at, slabs, chunks):
    count = own.shape[2] // (slabs * LANES)
    given = [] if modes is None else [modes]
    block = (ROWS, 2 * NBLK, 2 * slabs, LANES)
    return pl.pallas_call(
        lambda *refs: project_kernel(slabs, at, *refs),
        out_shape=jax.ShapeDtypeStruct((ROWS, 2 * NBLK, chunks, 2 * slabs, LANES), jnp.float32),
        in_specs=[pl.BlockSpec(memory_space=pltpu.VMEM)] * 3
        + [pl.BlockSpec(memory_space=pltpu.HBM)] * len(given),
        out_specs=pl.BlockSpec(memory_space=pltpu.HBM),
        input_output_aliases={3: 0} if given else {},
        scratch_shapes=[
            pltpu.VMEM((count, *block), jnp.float32),
            pltpu.SemaphoreType.DMA((count,)),
        ],
        compiler_params=pltpu.CompilerParams(vmem_limit_bytes=VMEM_BYTES),
        cost_estimate=pl.CostEstimate(
            flops=8 * own.size * NBLK, bytes_accessed=16 * own.size, transcendentals=0
        ),
        name="project",
    )(inv, own, far, *given)


def swap_bands(block):
    return lax.ppermute(block, "band", [(0, 1), (1, 0)])


def two_bands(snapshots, quad_weights, freq_bins, block_starts):
    slabs, cells = snapshots.shape[1:]
    chunks = cells // LANES
    count = 2 * slabs * cells * lax.axis_size("space")
    given = [
        pltpu.with_memory_space_constraint(array, pltpu.HBM)
        for array in (snapshots, quad_weights, freq_bins, block_starts)
    ]
    pieces = (chunks - 2, 1) if chunks > 2 else (1,)
    sends, owns, _ = spectra_call(*given, 0, (1,))
    fars = [swap_bands(sends[0])]
    later, owns_later, (gram_send,) = spectra_call(*given, 1, pieces, sends)
    far_gram = swap_bands(gram_send)
    fars += [swap_bands(send) for send in later]
    owns = [*owns, *owns_later]
    total = join_call(gram_call(owns, fars[0]), far_gram)
    for level in range(lax.axis_size("space").bit_length() - 1):
        total = total + from_partner(total, "space", level)
    inv, fac = factor_call(total, count)
    modes, at = None, 0
    for size, own, far in zip((1, *pieces), owns, fars):
        modes = project_call(inv, own, far, modes, at, slabs, chunks)
        at += size
    modes = modes.reshape(ROWS, 2, NBLK, chunks, 2 * slabs, LANES)
    modes = modes.transpose(0, 1, 2, 4, 3, 5).reshape(ROWS, 2, NBLK, 2 * slabs, cells)
    factor = fac[:, :NBLK].reshape(ROWS, 2, NBLK, NBLK)
    return (factor, modes)


def shards(snapshots, *others):
    fits = NFREQ == ROWS * lax.axis_size("band") == 2 * ROWS
    fits = fits and snapshots.shape[1] == SLABS // 2 and snapshots.shape[2] % LANES == 0
    fits = fits and snapshots.shape[2] > LANES and snapshots.shape[0] % LANES == 0
    return (two_bands if fits else any_bands)(snapshots, *others)


def solution(mesh):
    placed = (P(None, "band", "space"), P("band", "space"), P(), P())
    return jax.shard_map(
        shards,
        mesh=mesh,
        in_specs=placed,
        out_specs=(P("band", None, None, None), P("band", None, None, None, "space")),
        check_vma=False,
    )
```

```python
import math

import jax
import jax.numpy as jnp
from jax import lax
from jax.experimental import pallas as pl
from jax.experimental.pallas import tpu as pltpu
from jax.sharding import PartitionSpec as P

BLOCK = 256
NBLK = 8
NFREQ = 16
SLABS = 8
GAP_LOW = 64
GAP_HIGH = 192
LANES = 128
ROWS = 8
GROUPS = ((0, 1), (2, 3, 4), (5, 6, 7))
UNROLL = True
WINDOW = 3
PAD = 1
JOIN_FLOPS = 10**10
VMEM_BYTES = 24 * 1024 * 1024
PAIRS = [(a, b) for a in range(NBLK) for b in range(a, NBLK)]
ENTRIES = [(0, a, b) for a, b in PAIRS] + [(1, a, b) for a, b in PAIRS if a < b]


def from_partner(block, axis, apart):
    count = lax.axis_size(axis)
    route = []
    for low in range(count):
        high = low | 1 << apart
        if high != low and high < count:
            route += [(low, high), (high, low)]
    return lax.ppermute(block, axis, route)


def spectral_table(freq_bins, block_starts, total_times):
    moments = jnp.arange(total_times)
    offset = moments[None, :] - block_starts[:, None]
    inside = (offset >= 0) & (offset < BLOCK)
    position = offset.astype(jnp.float32)
    taper = 0.5 - 0.5 * jnp.cos(2.0 * math.pi * position / BLOCK)
    turns = jnp.mod(freq_bins[:, None, None] * offset[None, :, :], BLOCK).astype(jnp.float32)
    phase = 2.0 * math.pi * turns / BLOCK
    scaled = jnp.where(inside, taper, 0.0)[None] / math.sqrt(0.375 * BLOCK)
    table = jnp.stack([scaled * jnp.cos(phase), -scaled * jnp.sin(phase)], axis=1)
    return table.reshape(-1, total_times)


def spectra(snap_rows, weights, table):
    fluct = snap_rows - jnp.mean(snap_rows, axis=0, keepdims=True)
    coeffs = jnp.dot(
        table, fluct, precision=lax.Precision.HIGHEST, preferred_element_type=jnp.float32
    )
    return coeffs * jnp.sqrt(weights)[None, :]


def gram_local(coeffs, count):
    vectors = coeffs.reshape(coeffs.shape[0], 2 * coeffs.shape[2], -1)
    return jnp.einsum("fas,fbs->fab", vectors, vectors, precision=lax.Precision.HIGHEST) / count


def gram_split(moment):
    half = moment.shape[-1] // 2
    real_part = moment[:, :half, :half] + moment[:, half:, half:]
    imag_part = moment[:, :half, half:] - moment[:, half:, :half]
    return (real_part, imag_part)


def factor_pair(gram_real, gram_imag):
    order = gram_real.shape[-1]
    columns = jnp.arange(order)
    rows_real = []
    rows_imag = []
    for pivot_row in range(order):
        left_real = gram_real[:, pivot_row, :]
        left_imag = gram_imag[:, pivot_row, :]
        for earlier in range(pivot_row):
            coef_real = rows_real[earlier][:, pivot_row : pivot_row + 1]
            coef_imag = rows_imag[earlier][:, pivot_row : pivot_row + 1]
            left_real = left_real - (
                coef_real * rows_real[earlier] + coef_imag * rows_imag[earlier]
            )
            left_imag = left_imag - (
                coef_real * rows_imag[earlier] - coef_imag * rows_real[earlier]
            )
        pivot = jnp.sqrt(left_real[:, pivot_row : pivot_row + 1])
        rows_real.append(jnp.where(columns >= pivot_row, left_real / pivot, 0.0))
        rows_imag.append(jnp.where(columns > pivot_row, left_imag / pivot, 0.0))
    return (jnp.stack(rows_real, 1), jnp.stack(rows_imag, 1))


def invert_pair(fac_real, fac_imag):
    order = fac_real.shape[-1]
    identity = jnp.eye(order, dtype=fac_real.dtype)
    inv_real = [None] * order
    inv_imag = [None] * order
    for target in reversed(range(order)):
        acc_real = jnp.broadcast_to(identity[target], fac_real[:, 0, :].shape)
        acc_imag = jnp.zeros_like(acc_real)
        for later in range(target + 1, order):
            coef_real = fac_real[:, target, later : later + 1]
            coef_imag = fac_imag[:, target, later : later + 1]
            acc_real = acc_real - (coef_real * inv_real[later] - coef_imag * inv_imag[later])
            acc_imag = acc_imag - (coef_real * inv_imag[later] + coef_imag * inv_real[later])
        diagonal = fac_real[:, target, target : target + 1]
        inv_real[target] = acc_real / diagonal
        inv_imag[target] = acc_imag / diagonal
    return (jnp.stack(inv_real, 1), jnp.stack(inv_imag, 1))


def project(coeffs, inv_real, inv_imag):
    upper = jnp.stack([inv_real, inv_imag], 2)
    lower = jnp.stack([-inv_imag, inv_real], 2)
    kernel = jnp.stack([upper, lower], 1)
    flat = coeffs.reshape(coeffs.shape[0], 2, coeffs.shape[2], -1)
    result = jnp.einsum("fpacb,fpas->fcbs", kernel, flat, precision=lax.Precision.HIGHEST)
    return result.reshape(coeffs.shape)


def any_bands(snapshots, quad_weights, freq_bins, block_starts):
    total_times, local_slabs, slab_cells = snapshots.shape
    table = spectral_table(freq_bins, block_starts, total_times)
    coeffs = spectra(snapshots.reshape(total_times, -1), quad_weights.reshape(-1), table)
    coeffs = coeffs.reshape(NFREQ, 2, NBLK, local_slabs, slab_cells)
    count = SLABS * slab_cells * lax.axis_size("space")
    grouped = lax.all_to_all(coeffs, "band", split_axis=0, concat_axis=3, tiled=True)
    moment = gram_local(grouped, count)
    for level in range(lax.axis_size("space").bit_length() - 1):
        moment = moment + from_partner(moment, "space", level)
    fac_real, fac_imag = factor_pair(*gram_split(moment))
    modes = project(grouped, *invert_pair(fac_real, fac_imag))
    factor = jnp.stack([fac_real, fac_imag], 1)
    return (factor, modes)


def reach(total_times):
    last = total_times - BLOCK
    spans = []
    for j in range(NBLK):
        low = max(GAP_LOW * j, last - GAP_HIGH * (NBLK - 1 - j))
        high = min(GAP_HIGH * j, last - GAP_LOW * (NBLK - 1 - j))
        spans.append((low, high + BLOCK))
    return spans


def fill_table(freq_ref, start_ref, high_ref, low_ref):
    band = lax.axis_index("band")
    wide = BLOCK + LANES
    row = lax.broadcasted_iota(jnp.int32, (NFREQ, wide), 0)
    spot = lax.broadcasted_iota(jnp.int32, (NFREQ, wide), 1)
    bins = jnp.zeros((NFREQ, wide), jnp.int32)
    half = NFREQ // 2
    for r in range(NFREQ):
        owner = 1 - band if r < half else band
        bins = jnp.where(row == r, freq_ref[owner * half + r % half], bins)
    step = 2.0 * math.pi / BLOCK
    phase = ((bins * spot) & (BLOCK - 1)).astype(jnp.float32) * step
    taper = 0.5 - 0.5 * jnp.cos(spot.astype(jnp.float32) * step)
    scaled = jnp.where(spot < BLOCK, taper, 0.0) * (1.0 / math.sqrt(0.375 * BLOCK))
    parts = (scaled * jnp.cos(phase), -scaled * jnp.sin(phase))
    high_ref[...] = jnp.zeros_like(high_ref)
    low_ref[...] = jnp.zeros_like(low_ref)
    for j in range(NBLK):
        start = start_ref[j]
        shift = start % LANES
        place = pl.ds(pl.multiple_of(start - shift, LANES), wide)
        for p in range(2):
            moved = pltpu.roll(parts[p], shift, 1)
            high = moved.astype(jnp.bfloat16)
            low = (moved - high.astype(jnp.float32)).astype(jnp.bfloat16)
            rows = pl.ds((2 * j + p) * NFREQ, NFREQ)
            high_ref[rows, place] = high
            low_ref[rows, place] = low
    return [jnp.sum(part, axis=1, keepdims=True) for part in parts]


def coeff_chunk(flow_ref, total, base, high_ref, low_ref, fh_ref, fl_ref, acc_ref, slabs):
    apart = flow_ref.shape[0] // total
    per_block = 2 * NFREQ
    spans = reach(total)
    started = [False] * NBLK
    shift, left = [None] * slabs, [0.0] * slabs
    for i, t0 in enumerate(range(0, total, BLOCK)):
        t1 = min(t0 + BLOCK, total)
        for l in range(slabs):
            values = flow_ref[pl.ds(t0 * apart + base + l, t1 - t0, stride=apart), :]
            if i == 0:
                shift[l] = jnp.sum(values, axis=0, keepdims=True) * (1.0 / (t1 - t0))
            values = values - shift[l]
            left[l] += jnp.sum(values.reshape(-1, ROWS, LANES), axis=0)
            high = values.astype(jnp.bfloat16)
            cols = slice(l * LANES, (l + 1) * LANES)
            fh_ref[t0:t1, cols] = high
            fl_ref[t0:t1, cols] = (values - high.astype(jnp.float32)).astype(jnp.bfloat16)
    for i, t0 in enumerate(range(0, total, BLOCK)):
        t1 = min(t0 + BLOCK, total)
        hit = [j for j in range(NBLK) if spans[j][0] < t1 and spans[j][1] > t0]
        j0, j1 = min(hit), max(hit) + 1
        rows = slice(j0 * per_block, j1 * per_block)
        xh, xl = fh_ref[t0:t1, :], fl_ref[t0:t1, :]
        th, tl = high_ref[rows, t0:t1], low_ref[rows, t0:t1]
        part = jnp.dot(
            jnp.concatenate([th, tl, th], axis=1),
            jnp.concatenate([xh, xh, xl], axis=0),
            preferred_element_type=jnp.float32,
        )
        for j in range(j0, j1):
            own = slice(j * per_block, (j + 1) * per_block)
            piece = part[(j - j0) * per_block : (j - j0 + 1) * per_block]
            acc_ref[own, :] = acc_ref[own, :] + piece if started[j] else piece
            started[j] = True
    left = [jnp.sum(rest, axis=0, keepdims=True) * (1.0 / total) for rest in left]
    return jnp.concatenate(left, axis=1)


def store_chunk(acc_ref, left, sums, root, send_ref, own_ref):
    for p in range(2):
        mean_part = sums[p] * left
        for j in range(NBLK):
            jp = 2 * j + p
            piece = (acc_ref[jp * NFREQ : (jp + 1) * NFREQ, :] - mean_part) * root
            send_ref[jp] = piece[:ROWS]
            own_ref[jp] = piece[ROWS:]


def spectra_kernel(pieces, earlier, freq_hbm, start_hbm, weight_hbm, snap_ref, *rest):
    first = len(earlier)
    count, outs = sum(pieces), len(pieces)
    total, chunks, slabs, _ = snap_ref.shape
    sends, owns, rest = rest[:outs], rest[outs : 2 * outs], rest[2 * outs :]
    if earlier:
        gram_ref, *rest = rest
    freq_ref, start_ref, weight_ref, high_ref, low_ref, fh_ref, fl_ref, acc_ref, *rest = rest
    small_sems = rest[0]
    small = [
        pltpu.make_async_copy(source, target, small_sems.at[i])
        for i, (source, target) in enumerate(
            ((freq_hbm, freq_ref), (start_hbm, start_ref), (weight_hbm, weight_ref))
        )
    ]
    for copy in small:
        copy.start()
    held, sems = rest[1:]
    copies = [
        pltpu.make_async_copy(snap_ref.at[:, first + i], held.at[i], sems.at[i]) for i in range(count)
    ]
    for copy in copies[:WINDOW]:
        copy.start()
    for copy in small:
        copy.wait()
    sums = fill_table(freq_ref, start_ref, high_ref, low_ref)
    places = [(piece, at) for piece, size in enumerate(pieces) for at in range(size)]
    for i, (piece, at) in enumerate(places):
        weight = weight_ref[:, (first + i) * LANES : (first + i + 1) * LANES]
        root = jnp.concatenate([jnp.sqrt(weight[l : l + 1, :]) for l in range(slabs)], axis=1)
        copies[i].wait()
        if i + WINDOW < count:
            copies[i + WINDOW].start()
        flat = held.at[i].reshape(total * slabs, LANES)
        left = coeff_chunk(
            flat, total, 0, high_ref, low_ref, fh_ref, fl_ref, acc_ref, slabs
        )
        cols = slice(at * slabs * LANES, (at + 1) * slabs * LANES)
        store_chunk(acc_ref, left, sums, root, sends[piece].at[:, :, cols], owns[piece].at[:, :, cols])
    if earlier:
        gram_ref[...] = gram_sums([*earlier, *sends])


def spectra_call(snapshots, weights, freq_bins, block_starts, pieces, earlier=()):
    total, slabs, cells = snapshots.shape
    by_chunk = snapshots.reshape(total, slabs, -1, LANES).transpose(0, 2, 1, 3)
    cols = slabs * LANES
    count, outs, more = sum(pieces), len(pieces), len(earlier)
    shapes = [jax.ShapeDtypeStruct((2 * NBLK, ROWS, n * cols), jnp.float32) for n in pieces] * 2
    if more:
        shapes.append(jax.ShapeDtypeStruct((ROWS, LANES), jnp.float32))
    wide = -(-total // LANES) * LANES + LANES
    small = [pltpu.with_memory_space_constraint(v, pltpu.HBM) for v in (freq_bins, block_starts, weights)]
    if not more:
        by_chunk = pltpu.with_memory_space_constraint(by_chunk, pltpu.HBM)
    given = pl.pallas_call(
        lambda *refs: spectra_kernel(pieces, refs[4 : 4 + more], *refs[:4], *refs[4 + more :]),
        out_shape=tuple(shapes),
        in_specs=[pl.BlockSpec(memory_space=pltpu.HBM)] * 3
        + [pl.BlockSpec(memory_space=pltpu.VMEM if more else pltpu.HBM)]
        + [pl.BlockSpec(memory_space=pltpu.VMEM)] * more,
        out_specs=(pl.BlockSpec(memory_space=pltpu.VMEM),) * len(shapes),
        scratch_shapes=[
            pltpu.SMEM(freq_bins.shape, jnp.int32),
            pltpu.SMEM(block_starts.shape, jnp.int32),
            pltpu.VMEM(weights.shape, jnp.float32),
            pltpu.VMEM((2 * NBLK * NFREQ, wide), jnp.bfloat16),
            pltpu.VMEM((2 * NBLK * NFREQ, wide), jnp.bfloat16),
            pltpu.VMEM((total, cols), jnp.bfloat16),
            pltpu.VMEM((total, cols), jnp.bfloat16),
            pltpu.VMEM((2 * NBLK * NFREQ, cols), jnp.float32),
            pltpu.SemaphoreType.DMA((3,)),
            pltpu.VMEM((count, total, slabs, LANES), jnp.float32),
            pltpu.SemaphoreType.DMA((count,)),
        ],
        compiler_params=pltpu.CompilerParams(vmem_limit_bytes=VMEM_BYTES),
        cost_estimate=pl.CostEstimate(
            flops=6 * 2 * NBLK * NFREQ * total * count * cols,
            bytes_accessed=4 * (total + 2 * NBLK * NFREQ) * count * cols,
            transcendentals=0,
        ),
        name="spectra",
    )(*small, by_chunk, *earlier)
    return given[:outs], given[outs : 2 * outs], given[2 * outs :]


def lane_places(count):
    bits = LANES.bit_length() - 1
    used = count.bit_length() - 1
    lanes = []
    for e in range(count):
        lane = 0
        for level in range(used):
            if e >> (used - 1 - level) & 1:
                lane |= 1 << level
        lanes.append(lane)
    return lanes


def fold_lanes(terms):
    lane = lax.broadcasted_iota(jnp.int32, (ROWS, LANES), 1)
    apart = 1
    while len(terms) > 1:
        half = len(terms) // 2
        kept = (lane & apart) == 0
        merged = []
        for i in range(half):
            first, second = terms[i], terms[i + half]
            stay = jnp.where(kept, first, second)
            go = jnp.where(kept, second, first)
            fold = jnp.where(
                kept, pltpu.roll(go, LANES - apart, 1), pltpu.roll(go, apart, 1)
            )
            merged.append(stay + fold)
        terms = merged
        apart *= 2
    total = terms[0]
    while apart < LANES:
        total = total + pltpu.roll(total, apart, 1)
        apart *= 2
    return total


def gram_sums(blocks):
    sums = {}
    for group in GROUPS:
        keys = [key for key in ENTRIES if key[1] in group]
        carry = tuple(jnp.zeros((ROWS, LANES), jnp.float32) for _ in keys)
        for ref in blocks:

            def body(k, carry, ref=ref, group=group, keys=keys):
                cols = pl.ds(pl.multiple_of(k * LANES, LANES), LANES)
                re = {b: ref[2 * b, :, cols] for b in range(group[0], NBLK)}
                im = {b: ref[2 * b + 1, :, cols] for b in range(group[0], NBLK)}
                out = []
                for (kind, a, b), total in zip(keys, carry):
                    if kind == 0:
                        out.append(total + (re[a] * re[b] + im[a] * im[b]))
                    else:
                        out.append(total + (re[a] * im[b] - im[a] * re[b]))
                return tuple(out)

            carry = lax.fori_loop(0, ref.shape[2] // LANES, body, carry, unroll=UNROLL)
        sums.update(zip(keys, carry))
    return fold_lanes([sums[key] for key in ENTRIES])


def gram_kernel(count, *refs):
    refs[-1][...] = gram_sums(refs[:count])


def gram_call(blocks, after):
    return pl.pallas_call(
        lambda *refs: gram_kernel(len(blocks), *refs),
        out_shape=jax.ShapeDtypeStruct((ROWS, LANES), jnp.float32),
        in_specs=[pl.BlockSpec(memory_space=pltpu.VMEM)] * len(blocks)
        + [pl.BlockSpec(memory_space=pl.ANY)],
        out_specs=pl.BlockSpec(memory_space=pltpu.VMEM),
        compiler_params=pltpu.CompilerParams(vmem_limit_bytes=VMEM_BYTES),
        cost_estimate=pl.CostEstimate(
            flops=sum(block.size for block in blocks) * 4 * NBLK,
            bytes_accessed=4 * sum(block.size for block in blocks),
            transcendentals=0,
        ),
        name="gram",
    )(*blocks, after)


def join_kernel(own_ref, far_ref, out_ref):
    out_ref[...] = own_ref[...] + far_ref[...]


def join_call(own, far):
    return pl.pallas_call(
        join_kernel,
        out_shape=jax.ShapeDtypeStruct(own.shape, own.dtype),
        in_specs=[pl.BlockSpec(memory_space=pltpu.VMEM)] * 2,
        out_specs=pl.BlockSpec(memory_space=pltpu.VMEM),
        compiler_params=pltpu.CompilerParams(vmem_limit_bytes=VMEM_BYTES),
        cost_estimate=pl.CostEstimate(flops=JOIN_FLOPS, bytes_accessed=0, transcendentals=0),
        name="join",
    )(own, far)


def factor_kernel(count, sum_ref, inv_ref, fac_ref):
    total = sum_ref[...] * (1.0 / count)
    wide = lambda v: jnp.broadcast_to(v, (ROWS, LANES))
    gram = {
        key: wide(total[:, lane : lane + 1]) for key, lane in zip(ENTRIES, lane_places(len(ENTRIES)))
    }
    fac, recip = {}, []
    for r in range(NBLK):
        for c in range(r, NBLK):
            real = gram[0, r, c]
            imag = gram[1, r, c] if c > r else None
            for e in range(r):
                ar, ai = fac[0, e, r], fac[1, e, r]
                br, bi = fac[0, e, c], fac[1, e, c]
                real = real - (ar * br + ai * bi)
                if c > r:
                    imag = imag - (ar * bi - ai * br)
            if c == r:
                pivot = jnp.sqrt(real)
                fac[0, r, r] = pivot
                recip.append(1.0 / pivot)
            else:
                fac[0, r, c] = real * recip[r]
                fac[1, r, c] = imag * recip[r]
    inv = {}
    for b in range(NBLK):
        inv[0, b, b] = recip[b]
        for a in reversed(range(b)):
            real = imag = jnp.zeros((ROWS, LANES), jnp.float32)
            for k in range(a + 1, b + 1):
                cr, ci = fac[0, a, k], fac[1, a, k]
                real = real - cr * inv[0, k, b]
                imag = imag - ci * inv[0, k, b]
                if k < b:
                    real = real + ci * inv[1, k, b]
                    imag = imag - cr * inv[1, k, b]
            inv[0, a, b] = real * recip[a]
            inv[1, a, b] = imag * recip[a]
    for e, key in enumerate(ENTRIES):
        inv_ref[e] = inv[key]
    lane = lax.broadcasted_iota(jnp.int32, (ROWS, LANES), 1)
    for p in range(2):
        for a in range(NBLK):
            line = jnp.zeros((ROWS, LANES), jnp.float32)
            for b in range(a + p, NBLK):
                line = jnp.where(lane == b, fac[p, a, b], line)
            fac_ref[pl.ds(p * NBLK + a, ROWS, stride=2 * NBLK), :] = line


def factor_call(total, count):
    return pl.pallas_call(
        lambda *refs: factor_kernel(count, *refs),
        out_shape=(
            jax.ShapeDtypeStruct((len(ENTRIES), ROWS, LANES), jnp.float32),
            jax.ShapeDtypeStruct((ROWS * 2 * NBLK, LANES), jnp.float32),
        ),
        in_specs=[pl.BlockSpec(memory_space=pltpu.VMEM)],
        out_specs=(pl.BlockSpec(memory_space=pltpu.VMEM),) * 2,
        compiler_params=pltpu.CompilerParams(vmem_limit_bytes=VMEM_BYTES),
        name="factor",
    )(total)


def project_chunk(slabs, inv_ref, own_ref, far_ref, first, flat):
    band = lax.axis_index("band")
    per = flat.shape[0] // ROWS
    for side, ref in enumerate((own_ref, far_ref)):
        base = (band if side == 0 else 1 - band) * slabs
        for l0 in range(0, slabs, 2):
            both = range(l0, l0 + 2)
            cols = [pl.ds(pl.multiple_of(first + l * LANES, LANES), LANES) for l in both]
            re = [[ref[2 * a, :, at] for a in range(NBLK)] for at in cols]
            im = [[ref[2 * a + 1, :, at] for a in range(NBLK)] for at in cols]
            for b in range(NBLK):
                diagonal = inv_ref[ENTRIES.index((0, b, b))]
                real = [re[i][b] * diagonal for i in range(2)]
                imag = [im[i][b] * diagonal for i in range(2)]
                for a in range(b):
                    cr = inv_ref[ENTRIES.index((0, a, b))]
                    ci = inv_ref[ENTRIES.index((1, a, b))]
                    for i in range(2):
                        real[i] = real[i] + (re[i][a] * cr - im[i][a] * ci)
                        imag[i] = imag[i] + (re[i][a] * ci + im[i][a] * cr)
                for i in range(2):
                    for p, value in enumerate((real[i], imag[i])):
                        line = (p * NBLK + b) * 2 * slabs + base + l0 + i
                        flat[pl.ds(line, ROWS, stride=per), :] = value


def project_kernel(slabs, at, inv_ref, own_ref, far_ref, *rest):
    out_ref, held, sems = rest[-3:]
    count = held.shape[0]
    per = (2 * NBLK + PAD) * 2 * slabs

    def copy_of(i):
        return pltpu.make_async_copy(held.at[i, :, : 2 * NBLK], out_ref.at[:, :, at + i], sems.at[i])

    def body(i, _):
        flat = held.at[i].reshape(ROWS * per, LANES)
        project_chunk(slabs, inv_ref, own_ref, far_ref, i * slabs * LANES, flat)
        copy_of(i).start()
        return 0

    lax.fori_loop(0, count, body, 0)
    for i in range(count):
        copy_of(i).wait()


def project_call(inv, own, far, modes, at, slabs, chunks):
    count = own.shape[2] // (slabs * LANES)
    given = [] if modes is None else [modes]
    return pl.pallas_call(
        lambda *refs: project_kernel(slabs, at, *refs),
        out_shape=jax.ShapeDtypeStruct((ROWS, 2 * NBLK, chunks, 2 * slabs, LANES), jnp.float32),
        in_specs=[pl.BlockSpec(memory_space=pltpu.VMEM)] * 3
        + [pl.BlockSpec(memory_space=pltpu.HBM)] * len(given),
        out_specs=pl.BlockSpec(memory_space=pltpu.HBM),
        input_output_aliases={3: 0} if given else {},
        scratch_shapes=[
            pltpu.VMEM((count, ROWS, 2 * NBLK + PAD, 2 * slabs, LANES), jnp.float32),
            pltpu.SemaphoreType.DMA((count,)),
        ],
        compiler_params=pltpu.CompilerParams(vmem_limit_bytes=VMEM_BYTES),
        cost_estimate=pl.CostEstimate(
            flops=8 * own.size * NBLK, bytes_accessed=16 * own.size, transcendentals=0
        ),
        name="project",
    )(inv, own, far, *given)


def swap_bands(block):
    return lax.ppermute(block, "band", [(0, 1), (1, 0)])


def two_bands(snapshots, quad_weights, freq_bins, block_starts):
    slabs, cells = snapshots.shape[1:]
    chunks = cells // LANES
    count = 2 * slabs * cells * lax.axis_size("space")
    given = (snapshots, quad_weights, freq_bins, block_starts)
    pieces = (chunks - 2, 1) if chunks > 2 else (1,)
    sends, owns, _ = spectra_call(*given, (1,))
    fars = [swap_bands(sends[0])]
    later, owns_later, (gram_send,) = spectra_call(*given, pieces, sends)
    far_gram = swap_bands(gram_send)
    fars += [swap_bands(send) for send in later]
    owns = [*owns, *owns_later]
    total = join_call(gram_call(owns, fars[0]), far_gram)
    for level in range(lax.axis_size("space").bit_length() - 1):
        total = total + from_partner(total, "space", level)
    inv, fac = factor_call(total, count)
    modes, at = None, 0
    for size, own, far in zip((1, *pieces), owns, fars):
        modes = project_call(inv, own, far, modes, at, slabs, chunks)
        at += size
    modes = modes.reshape(ROWS, 2, NBLK, chunks, 2 * slabs, LANES)
    modes = modes.transpose(0, 1, 2, 4, 3, 5).reshape(ROWS, 2, NBLK, 2 * slabs, cells)
    factor = fac[:, :NBLK].reshape(ROWS, 2, NBLK, NBLK)
    return (factor, modes)


def shards(snapshots, *others):
    fits = NFREQ == ROWS * lax.axis_size("band") == 2 * ROWS
    fits = fits and snapshots.shape[1] == SLABS // 2 and snapshots.shape[2] % LANES == 0
    fits = fits and snapshots.shape[2] > LANES and snapshots.shape[0] % LANES == 0
    return (two_bands if fits else any_bands)(snapshots, *others)


def solution(mesh):
    placed = (P(None, "band", "space"), P("band", "space"), P(), P())
    return jax.shard_map(
        shards,
        mesh=mesh,
        in_specs=placed,
        out_specs=(P("band", None, None, None), P("band", None, None, None, "space")),
        check_vma=False,
    )
```

```python
import math

import jax
import jax.numpy as jnp
from jax import lax
from jax.experimental import pallas as pl
from jax.experimental.pallas import tpu as pltpu
from jax.sharding import PartitionSpec as P

BLOCK = 256
NBLK = 8
NFREQ = 16
SLABS = 8
GAP_LOW = 64
GAP_HIGH = 192
LANES = 128
ROWS = 8
GROUPS = ((0, 1), (2, 3, 4), (5, 6, 7))
UNROLL = True
WINDOW = 3
PAD = 1
JOIN_FLOPS = 10**10
VMEM_BYTES = 24 * 1024 * 1024
PAIRS = [(a, b) for a in range(NBLK) for b in range(a, NBLK)]
ENTRIES = [(0, a, b) for a, b in PAIRS] + [(1, a, b) for a, b in PAIRS if a < b]


def from_partner(block, axis, apart):
    count = lax.axis_size(axis)
    route = []
    for low in range(count):
        high = low | 1 << apart
        if high != low and high < count:
            route += [(low, high), (high, low)]
    return lax.ppermute(block, axis, route)


def spectral_table(freq_bins, block_starts, total_times):
    moments = jnp.arange(total_times)
    offset = moments[None, :] - block_starts[:, None]
    inside = (offset >= 0) & (offset < BLOCK)
    position = offset.astype(jnp.float32)
    taper = 0.5 - 0.5 * jnp.cos(2.0 * math.pi * position / BLOCK)
    turns = jnp.mod(freq_bins[:, None, None] * offset[None, :, :], BLOCK).astype(jnp.float32)
    phase = 2.0 * math.pi * turns / BLOCK
    scaled = jnp.where(inside, taper, 0.0)[None] / math.sqrt(0.375 * BLOCK)
    table = jnp.stack([scaled * jnp.cos(phase), -scaled * jnp.sin(phase)], axis=1)
    return table.reshape(-1, total_times)


def spectra(snap_rows, weights, table):
    fluct = snap_rows - jnp.mean(snap_rows, axis=0, keepdims=True)
    coeffs = jnp.dot(
        table, fluct, precision=lax.Precision.HIGHEST, preferred_element_type=jnp.float32
    )
    return coeffs * jnp.sqrt(weights)[None, :]


def gram_local(coeffs, count):
    vectors = coeffs.reshape(coeffs.shape[0], 2 * coeffs.shape[2], -1)
    return jnp.einsum("fas,fbs->fab", vectors, vectors, precision=lax.Precision.HIGHEST) / count


def gram_split(moment):
    half = moment.shape[-1] // 2
    real_part = moment[:, :half, :half] + moment[:, half:, half:]
    imag_part = moment[:, :half, half:] - moment[:, half:, :half]
    return (real_part, imag_part)


def factor_pair(gram_real, gram_imag):
    order = gram_real.shape[-1]
    columns = jnp.arange(order)
    rows_real = []
    rows_imag = []
    for pivot_row in range(order):
        left_real = gram_real[:, pivot_row, :]
        left_imag = gram_imag[:, pivot_row, :]
        for earlier in range(pivot_row):
            coef_real = rows_real[earlier][:, pivot_row : pivot_row + 1]
            coef_imag = rows_imag[earlier][:, pivot_row : pivot_row + 1]
            left_real = left_real - (
                coef_real * rows_real[earlier] + coef_imag * rows_imag[earlier]
            )
            left_imag = left_imag - (
                coef_real * rows_imag[earlier] - coef_imag * rows_real[earlier]
            )
        pivot = jnp.sqrt(left_real[:, pivot_row : pivot_row + 1])
        rows_real.append(jnp.where(columns >= pivot_row, left_real / pivot, 0.0))
        rows_imag.append(jnp.where(columns > pivot_row, left_imag / pivot, 0.0))
    return (jnp.stack(rows_real, 1), jnp.stack(rows_imag, 1))


def invert_pair(fac_real, fac_imag):
    order = fac_real.shape[-1]
    identity = jnp.eye(order, dtype=fac_real.dtype)
    inv_real = [None] * order
    inv_imag = [None] * order
    for target in reversed(range(order)):
        acc_real = jnp.broadcast_to(identity[target], fac_real[:, 0, :].shape)
        acc_imag = jnp.zeros_like(acc_real)
        for later in range(target + 1, order):
            coef_real = fac_real[:, target, later : later + 1]
            coef_imag = fac_imag[:, target, later : later + 1]
            acc_real = acc_real - (coef_real * inv_real[later] - coef_imag * inv_imag[later])
            acc_imag = acc_imag - (coef_real * inv_imag[later] + coef_imag * inv_real[later])
        diagonal = fac_real[:, target, target : target + 1]
        inv_real[target] = acc_real / diagonal
        inv_imag[target] = acc_imag / diagonal
    return (jnp.stack(inv_real, 1), jnp.stack(inv_imag, 1))


def project(coeffs, inv_real, inv_imag):
    upper = jnp.stack([inv_real, inv_imag], 2)
    lower = jnp.stack([-inv_imag, inv_real], 2)
    kernel = jnp.stack([upper, lower], 1)
    flat = coeffs.reshape(coeffs.shape[0], 2, coeffs.shape[2], -1)
    result = jnp.einsum("fpacb,fpas->fcbs", kernel, flat, precision=lax.Precision.HIGHEST)
    return result.reshape(coeffs.shape)


def any_bands(snapshots, quad_weights, freq_bins, block_starts):
    total_times, local_slabs, slab_cells = snapshots.shape
    table = spectral_table(freq_bins, block_starts, total_times)
    coeffs = spectra(snapshots.reshape(total_times, -1), quad_weights.reshape(-1), table)
    coeffs = coeffs.reshape(NFREQ, 2, NBLK, local_slabs, slab_cells)
    count = SLABS * slab_cells * lax.axis_size("space")
    grouped = lax.all_to_all(coeffs, "band", split_axis=0, concat_axis=3, tiled=True)
    moment = gram_local(grouped, count)
    for level in range(lax.axis_size("space").bit_length() - 1):
        moment = moment + from_partner(moment, "space", level)
    fac_real, fac_imag = factor_pair(*gram_split(moment))
    modes = project(grouped, *invert_pair(fac_real, fac_imag))
    factor = jnp.stack([fac_real, fac_imag], 1)
    return (factor, modes)


def reach(total_times):
    last = total_times - BLOCK
    spans = []
    for j in range(NBLK):
        low = max(GAP_LOW * j, last - GAP_HIGH * (NBLK - 1 - j))
        high = min(GAP_HIGH * j, last - GAP_LOW * (NBLK - 1 - j))
        spans.append((low, high + BLOCK))
    return spans


def fill_table(freq_ref, start_ref, high_ref, low_ref):
    band = lax.axis_index("band")
    wide = BLOCK + LANES
    row = lax.broadcasted_iota(jnp.int32, (NFREQ, wide), 0)
    spot = lax.broadcasted_iota(jnp.int32, (NFREQ, wide), 1)
    bins = jnp.zeros((NFREQ, wide), jnp.int32)
    half = NFREQ // 2
    for r in range(NFREQ):
        owner = 1 - band if r < half else band
        bins = jnp.where(row == r, freq_ref[owner * half + r % half], bins)
    step = 2.0 * math.pi / BLOCK
    phase = ((bins * spot) & (BLOCK - 1)).astype(jnp.float32) * step
    taper = 0.5 - 0.5 * jnp.cos(spot.astype(jnp.float32) * step)
    scaled = jnp.where(spot < BLOCK, taper, 0.0) * (1.0 / math.sqrt(0.375 * BLOCK))
    parts = (scaled * jnp.cos(phase), -scaled * jnp.sin(phase))
    high_ref[...] = jnp.zeros_like(high_ref)
    low_ref[...] = jnp.zeros_like(low_ref)
    for j in range(NBLK):
        start = start_ref[j]
        shift = start % LANES
        place = pl.ds(pl.multiple_of(start - shift, LANES), wide)
        for p in range(2):
            moved = pltpu.roll(parts[p], shift, 1)
            high = moved.astype(jnp.bfloat16)
            low = (moved - high.astype(jnp.float32)).astype(jnp.bfloat16)
            rows = pl.ds((2 * j + p) * NFREQ, NFREQ)
            high_ref[rows, place] = high
            low_ref[rows, place] = low
    return [jnp.sum(part, axis=1, keepdims=True) for part in parts]


def coeff_chunk(flow_ref, total, base, high_ref, low_ref, fh_ref, fl_ref, acc_ref, slabs):
    apart = flow_ref.shape[0] // total
    per_block = 2 * NFREQ
    spans = reach(total)
    started = [False] * NBLK
    shift, left = [None] * slabs, [0.0] * slabs
    for i, t0 in enumerate(range(0, total, BLOCK)):
        t1 = min(t0 + BLOCK, total)
        for l in range(slabs):
            values = flow_ref[pl.ds(t0 * apart + base + l, t1 - t0, stride=apart), :]
            if i == 0:
                shift[l] = jnp.sum(values, axis=0, keepdims=True) * (1.0 / (t1 - t0))
            values = values - shift[l]
            left[l] += jnp.sum(values.reshape(-1, ROWS, LANES), axis=0)
            high = values.astype(jnp.bfloat16)
            cols = slice(l * LANES, (l + 1) * LANES)
            fh_ref[t0:t1, cols] = high
            fl_ref[t0:t1, cols] = (values - high.astype(jnp.float32)).astype(jnp.bfloat16)
    for i, t0 in enumerate(range(0, total, BLOCK)):
        t1 = min(t0 + BLOCK, total)
        hit = [j for j in range(NBLK) if spans[j][0] < t1 and spans[j][1] > t0]
        j0, j1 = min(hit), max(hit) + 1
        rows = slice(j0 * per_block, j1 * per_block)
        xh, xl = fh_ref[t0:t1, :], fl_ref[t0:t1, :]
        th, tl = high_ref[rows, t0:t1], low_ref[rows, t0:t1]
        part = jnp.dot(
            jnp.concatenate([th, tl, th], axis=1),
            jnp.concatenate([xh, xh, xl], axis=0),
            preferred_element_type=jnp.float32,
        )
        for j in range(j0, j1):
            own = slice(j * per_block, (j + 1) * per_block)
            piece = part[(j - j0) * per_block : (j - j0 + 1) * per_block]
            acc_ref[own, :] = acc_ref[own, :] + piece if started[j] else piece
            started[j] = True
    left = [jnp.sum(rest, axis=0, keepdims=True) * (1.0 / total) for rest in left]
    return jnp.concatenate(left, axis=1)


def store_chunk(acc_ref, left, sums, root, send_ref, own_ref):
    for p in range(2):
        mean_part = sums[p] * left
        for j in range(NBLK):
            jp = 2 * j + p
            piece = (acc_ref[jp * NFREQ : (jp + 1) * NFREQ, :] - mean_part) * root
            send_ref[jp] = piece[:ROWS]
            own_ref[jp] = piece[ROWS:]


def spectra_kernel(pieces, earlier, freq_hbm, start_hbm, weight_hbm, snap_ref, *rest):
    first = len(earlier)
    count, outs = sum(pieces), len(pieces)
    total, chunks, slabs, _ = snap_ref.shape
    sends, owns, rest = rest[:outs], rest[outs : 2 * outs], rest[2 * outs :]
    if earlier:
        gram_ref, *rest = rest
    freq_ref, start_ref, weight_ref, high_ref, low_ref, fh_ref, fl_ref, acc_ref, *rest = rest
    small_sems = rest[0]
    small = [
        pltpu.make_async_copy(source, target, small_sems.at[i])
        for i, (source, target) in enumerate(
            ((freq_hbm, freq_ref), (start_hbm, start_ref), (weight_hbm, weight_ref))
        )
    ]
    for copy in small:
        copy.start()
    held, sems = rest[1:]
    copies = [
        pltpu.make_async_copy(snap_ref.at[:, first + i], held.at[i], sems.at[i]) for i in range(count)
    ]
    for copy in copies[:WINDOW]:
        copy.start()
    for copy in small:
        copy.wait()
    sums = fill_table(freq_ref, start_ref, high_ref, low_ref)
    places = [(piece, at) for piece, size in enumerate(pieces) for at in range(size)]
    for i, (piece, at) in enumerate(places):
        weight = weight_ref[:, (first + i) * LANES : (first + i + 1) * LANES]
        root = jnp.concatenate([jnp.sqrt(weight[l : l + 1, :]) for l in range(slabs)], axis=1)
        copies[i].wait()
        if i + WINDOW < count:
            copies[i + WINDOW].start()
        flat = held.at[i].reshape(total * slabs, LANES)
        left = coeff_chunk(
            flat, total, 0, high_ref, low_ref, fh_ref, fl_ref, acc_ref, slabs
        )
        cols = slice(at * slabs * LANES, (at + 1) * slabs * LANES)
        store_chunk(acc_ref, left, sums, root, sends[piece].at[:, :, cols], owns[piece].at[:, :, cols])
    if earlier:
        gram_ref[...] = gram_sums([*earlier, *sends])


def spectra_call(snapshots, weights, freq_bins, block_starts, pieces, earlier=()):
    total, slabs, cells = snapshots.shape
    by_chunk = snapshots.reshape(total, slabs, -1, LANES).transpose(0, 2, 1, 3)
    cols = slabs * LANES
    count, outs, more = sum(pieces), len(pieces), len(earlier)
    shapes = [jax.ShapeDtypeStruct((2 * NBLK, ROWS, n * cols), jnp.float32) for n in pieces] * 2
    if more:
        shapes.append(jax.ShapeDtypeStruct((ROWS, LANES), jnp.float32))
    wide = -(-total // LANES) * LANES + LANES
    small = [pltpu.with_memory_space_constraint(v, pltpu.HBM) for v in (freq_bins, block_starts, weights)]
    if not more:
        by_chunk = pltpu.with_memory_space_constraint(by_chunk, pltpu.HBM)
    given = pl.pallas_call(
        lambda *refs: spectra_kernel(pieces, refs[4 : 4 + more], *refs[:4], *refs[4 + more :]),
        out_shape=tuple(shapes),
        in_specs=[pl.BlockSpec(memory_space=pltpu.HBM)] * 3
        + [pl.BlockSpec(memory_space=pltpu.VMEM if more else pltpu.HBM)]
        + [pl.BlockSpec(memory_space=pltpu.VMEM)] * more,
        out_specs=(pl.BlockSpec(memory_space=pltpu.VMEM),) * len(shapes),
        scratch_shapes=[
            pltpu.SMEM(freq_bins.shape, jnp.int32),
            pltpu.SMEM(block_starts.shape, jnp.int32),
            pltpu.VMEM(weights.shape, jnp.float32),
            pltpu.VMEM((2 * NBLK * NFREQ, wide), jnp.bfloat16),
            pltpu.VMEM((2 * NBLK * NFREQ, wide), jnp.bfloat16),
            pltpu.VMEM((total, cols), jnp.bfloat16),
            pltpu.VMEM((total, cols), jnp.bfloat16),
            pltpu.VMEM((2 * NBLK * NFREQ, cols), jnp.float32),
            pltpu.SemaphoreType.DMA((3,)),
            pltpu.VMEM((count, total, slabs, LANES), jnp.float32),
            pltpu.SemaphoreType.DMA((count,)),
        ],
        compiler_params=pltpu.CompilerParams(vmem_limit_bytes=VMEM_BYTES),
        cost_estimate=pl.CostEstimate(
            flops=6 * 2 * NBLK * NFREQ * total * count * cols,
            bytes_accessed=4 * (total + 2 * NBLK * NFREQ) * count * cols,
            transcendentals=0,
        ),
        name="spectra",
    )(*small, by_chunk, *earlier)
    return given[:outs], given[outs : 2 * outs], given[2 * outs :]


def lane_places(count):
    bits = LANES.bit_length() - 1
    used = count.bit_length() - 1
    lanes = []
    for e in range(count):
        lane = 0
        for level in range(used):
            if e >> (used - 1 - level) & 1:
                lane |= 1 << level
        lanes.append(lane)
    return lanes


def fold_lanes(terms):
    lane = lax.broadcasted_iota(jnp.int32, (ROWS, LANES), 1)
    apart = 1
    while len(terms) > 1:
        half = len(terms) // 2
        kept = (lane & apart) == 0
        merged = []
        for i in range(half):
            first, second = terms[i], terms[i + half]
            stay = jnp.where(kept, first, second)
            go = jnp.where(kept, second, first)
            fold = jnp.where(
                kept, pltpu.roll(go, LANES - apart, 1), pltpu.roll(go, apart, 1)
            )
            merged.append(stay + fold)
        terms = merged
        apart *= 2
    total = terms[0]
    while apart < LANES:
        total = total + pltpu.roll(total, apart, 1)
        apart *= 2
    return total


def gram_sums(blocks):
    sums = {}
    for group in GROUPS:
        keys = [key for key in ENTRIES if key[1] in group]
        carry = tuple(jnp.zeros((ROWS, LANES), jnp.float32) for _ in keys)
        for ref in blocks:

            def body(k, carry, ref=ref, group=group, keys=keys):
                cols = pl.ds(pl.multiple_of(k * LANES, LANES), LANES)
                re = {b: ref[2 * b, :, cols] for b in range(group[0], NBLK)}
                im = {b: ref[2 * b + 1, :, cols] for b in range(group[0], NBLK)}
                out = []
                for (kind, a, b), total in zip(keys, carry):
                    if kind == 0:
                        out.append(total + (re[a] * re[b] + im[a] * im[b]))
                    else:
                        out.append(total + (re[a] * im[b] - im[a] * re[b]))
                return tuple(out)

            carry = lax.fori_loop(0, ref.shape[2] // LANES, body, carry, unroll=UNROLL)
        sums.update(zip(keys, carry))
    return fold_lanes([sums[key] for key in ENTRIES])


def gram_kernel(count, *refs):
    refs[-2][...] = gram_sums(refs[:count])


def gram_call(blocks, after, passed):
    count = len(blocks)
    return pl.pallas_call(
        lambda *refs: gram_kernel(count, *refs),
        out_shape=(
            jax.ShapeDtypeStruct((ROWS, LANES), jnp.float32),
            jax.ShapeDtypeStruct(passed.shape, passed.dtype),
        ),
        in_specs=[pl.BlockSpec(memory_space=pltpu.VMEM)] * count
        + [pl.BlockSpec(memory_space=pl.ANY)] * 2,
        out_specs=(pl.BlockSpec(memory_space=pltpu.VMEM), pl.BlockSpec(memory_space=pl.ANY)),
        input_output_aliases={count + 1: 1},
        compiler_params=pltpu.CompilerParams(vmem_limit_bytes=VMEM_BYTES),
        cost_estimate=pl.CostEstimate(
            flops=sum(block.size for block in blocks) * 4 * NBLK,
            bytes_accessed=4 * sum(block.size for block in blocks),
            transcendentals=0,
        ),
        name="gram",
    )(*blocks, after, passed)


def join_kernel(own_ref, far_ref, out_ref):
    out_ref[...] = own_ref[...] + far_ref[...]


def join_call(own, far):
    return pl.pallas_call(
        join_kernel,
        out_shape=jax.ShapeDtypeStruct(own.shape, own.dtype),
        in_specs=[pl.BlockSpec(memory_space=pltpu.VMEM)] * 2,
        out_specs=pl.BlockSpec(memory_space=pltpu.VMEM),
        compiler_params=pltpu.CompilerParams(vmem_limit_bytes=VMEM_BYTES),
        cost_estimate=pl.CostEstimate(flops=JOIN_FLOPS, bytes_accessed=0, transcendentals=0),
        name="join",
    )(own, far)


def factor_kernel(count, sum_ref, inv_ref, fac_ref):
    total = sum_ref[...] * (1.0 / count)
    wide = lambda v: jnp.broadcast_to(v, (ROWS, LANES))
    gram = {
        key: wide(total[:, lane : lane + 1]) for key, lane in zip(ENTRIES, lane_places(len(ENTRIES)))
    }
    fac, recip = {}, []
    for r in range(NBLK):
        for c in range(r, NBLK):
            real = gram[0, r, c]
            imag = gram[1, r, c] if c > r else None
            for e in range(r):
                ar, ai = fac[0, e, r], fac[1, e, r]
                br, bi = fac[0, e, c], fac[1, e, c]
                real = real - (ar * br + ai * bi)
                if c > r:
                    imag = imag - (ar * bi - ai * br)
            if c == r:
                pivot = jnp.sqrt(real)
                fac[0, r, r] = pivot
                recip.append(1.0 / pivot)
            else:
                fac[0, r, c] = real * recip[r]
                fac[1, r, c] = imag * recip[r]
    inv = {}
    for b in range(NBLK):
        inv[0, b, b] = recip[b]
        for a in reversed(range(b)):
            real = imag = jnp.zeros((ROWS, LANES), jnp.float32)
            for k in range(a + 1, b + 1):
                cr, ci = fac[0, a, k], fac[1, a, k]
                real = real - cr * inv[0, k, b]
                imag = imag - ci * inv[0, k, b]
                if k < b:
                    real = real + ci * inv[1, k, b]
                    imag = imag - cr * inv[1, k, b]
            inv[0, a, b] = real * recip[a]
            inv[1, a, b] = imag * recip[a]
    for e, key in enumerate(ENTRIES):
        inv_ref[e] = inv[key]
    lane = lax.broadcasted_iota(jnp.int32, (ROWS, LANES), 1)
    for p in range(2):
        for a in range(NBLK):
            line = jnp.zeros((ROWS, LANES), jnp.float32)
            for b in range(a + p, NBLK):
                line = jnp.where(lane == b, fac[p, a, b], line)
            fac_ref[pl.ds(p * NBLK + a, ROWS, stride=2 * NBLK), :] = line


def factor_call(total, count):
    return pl.pallas_call(
        lambda *refs: factor_kernel(count, *refs),
        out_shape=(
            jax.ShapeDtypeStruct((len(ENTRIES), ROWS, LANES), jnp.float32),
            jax.ShapeDtypeStruct((ROWS * 2 * NBLK, LANES), jnp.float32),
        ),
        in_specs=[pl.BlockSpec(memory_space=pltpu.VMEM)],
        out_specs=(pl.BlockSpec(memory_space=pltpu.VMEM),) * 2,
        compiler_params=pltpu.CompilerParams(vmem_limit_bytes=VMEM_BYTES),
        name="factor",
    )(total)


def project_chunk(slabs, inv_ref, own_ref, far_ref, first, flat):
    band = lax.axis_index("band")
    per = flat.shape[0] // ROWS
    for side, ref in enumerate((own_ref, far_ref)):
        base = (band if side == 0 else 1 - band) * slabs
        for l0 in range(0, slabs, 2):
            both = range(l0, l0 + 2)
            cols = [pl.ds(pl.multiple_of(first + l * LANES, LANES), LANES) for l in both]
            re = [[ref[2 * a, :, at] for a in range(NBLK)] for at in cols]
            im = [[ref[2 * a + 1, :, at] for a in range(NBLK)] for at in cols]
            for b in range(NBLK):
                diagonal = inv_ref[ENTRIES.index((0, b, b))]
                real = [re[i][b] * diagonal for i in range(2)]
                imag = [im[i][b] * diagonal for i in range(2)]
                for a in range(b):
                    cr = inv_ref[ENTRIES.index((0, a, b))]
                    ci = inv_ref[ENTRIES.index((1, a, b))]
                    for i in range(2):
                        real[i] = real[i] + (re[i][a] * cr - im[i][a] * ci)
                        imag[i] = imag[i] + (re[i][a] * ci + im[i][a] * cr)
                for i in range(2):
                    for p, value in enumerate((real[i], imag[i])):
                        line = (p * NBLK + b) * 2 * slabs + base + l0 + i
                        flat[pl.ds(line, ROWS, stride=per), :] = value


def project_kernel(slabs, at, sizes, inv_ref, *refs):
    out_ref, held, sems = refs[-3:]
    per = (2 * NBLK + PAD) * 2 * slabs

    def copy_of(i):
        return pltpu.make_async_copy(held.at[i, :, : 2 * NBLK], out_ref.at[:, :, at + i], sems.at[i])

    done = 0
    for piece, size in enumerate(sizes):
        own_ref, far_ref = refs[2 * piece : 2 * piece + 2]

        def body(i, _, own_ref=own_ref, far_ref=far_ref, done=done):
            flat = held.at[done + i].reshape(ROWS * per, LANES)
            project_chunk(slabs, inv_ref, own_ref, far_ref, i * slabs * LANES, flat)
            copy_of(done + i).start()
            return 0

        lax.fori_loop(0, size, body, 0)
        done += size
    for i in range(done):
        copy_of(i).wait()


def project_call(inv, pairs, modes, at, slabs, chunks):
    sizes = [own.shape[2] // (slabs * LANES) for own, _ in pairs]
    count = sum(sizes)
    given = [] if modes is None else [modes]
    arrays = [array for pair in pairs for array in pair]
    values = sum(array.size for array in arrays)
    return pl.pallas_call(
        lambda *refs: project_kernel(slabs, at, sizes, *refs),
        out_shape=jax.ShapeDtypeStruct((ROWS, 2 * NBLK, chunks, 2 * slabs, LANES), jnp.float32),
        in_specs=[pl.BlockSpec(memory_space=pltpu.VMEM)] * (1 + len(arrays))
        + [pl.BlockSpec(memory_space=pltpu.HBM)] * len(given),
        out_specs=pl.BlockSpec(memory_space=pltpu.HBM),
        input_output_aliases={1 + len(arrays): 0} if given else {},
        scratch_shapes=[
            pltpu.VMEM((count, ROWS, 2 * NBLK + PAD, 2 * slabs, LANES), jnp.float32),
            pltpu.SemaphoreType.DMA((count,)),
        ],
        compiler_params=pltpu.CompilerParams(vmem_limit_bytes=VMEM_BYTES),
        cost_estimate=pl.CostEstimate(
            flops=4 * values * NBLK, bytes_accessed=8 * values, transcendentals=0
        ),
        name="project",
    )(inv, *arrays, *given)


def swap_bands(block):
    return lax.ppermute(block, "band", [(0, 1), (1, 0)])


def two_bands(snapshots, quad_weights, freq_bins, block_starts):
    slabs, cells = snapshots.shape[1:]
    chunks = cells // LANES
    count = 2 * slabs * cells * lax.axis_size("space")
    given = (snapshots, quad_weights, freq_bins, block_starts)
    (send_a,), (own_a,), _ = spectra_call(*given, (1,))
    far_a = swap_bands(send_a)
    (send_b, send_c), (own_b, own_c), (gram_send,) = spectra_call(*given, (chunks - 2, 1), [send_a])
    far_gram = swap_bands(gram_send)
    far_b = swap_bands(send_b)
    gram_own, send_c = gram_call([own_a, own_b, own_c], far_a, send_c)
    far_c = swap_bands(send_c)
    total = join_call(gram_own, far_gram)
    for level in range(lax.axis_size("space").bit_length() - 1):
        total = total + from_partner(total, "space", level)
    inv, fac = factor_call(total, count)
    modes = project_call(inv, [(own_a, far_a), (own_b, far_b)], None, 0, slabs, chunks)
    modes = project_call(inv, [(own_c, far_c)], modes, chunks - 1, slabs, chunks)
    modes = modes.reshape(ROWS, 2, NBLK, chunks, 2 * slabs, LANES)
    modes = modes.transpose(0, 1, 2, 4, 3, 5).reshape(ROWS, 2, NBLK, 2 * slabs, cells)
    factor = fac[:, :NBLK].reshape(ROWS, 2, NBLK, NBLK)
    return (factor, modes)


def shards(snapshots, *others):
    fits = NFREQ == ROWS * lax.axis_size("band") == 2 * ROWS
    fits = fits and snapshots.shape[1] == SLABS // 2 and snapshots.shape[2] % LANES == 0
    fits = fits and snapshots.shape[2] > 2 * LANES and snapshots.shape[0] % LANES == 0
    return (two_bands if fits else any_bands)(snapshots, *others)


def solution(mesh):
    placed = (P(None, "band", "space"), P("band", "space"), P(), P())
    return jax.shard_map(
        shards,
        mesh=mesh,
        in_specs=placed,
        out_specs=(P("band", None, None, None), P("band", None, None, None, "space")),
        check_vma=False,
    )
```

```python
import math

import jax
import jax.numpy as jnp
from jax import lax
from jax.experimental import pallas as pl
from jax.experimental.pallas import tpu as pltpu
from jax.sharding import PartitionSpec as P

BLOCK = 256
NBLK = 8
NFREQ = 16
SLABS = 8
GAP_LOW = 64
GAP_HIGH = 192
LANES = 128
ROWS = 8
GROUPS = ((0, 1), (2, 3, 4), (5, 6, 7))
PAD = 1
JOIN_FLOPS = 10**10
VMEM_BYTES = 24 * 1024 * 1024
PAIRS = [(a, b) for a in range(NBLK) for b in range(a, NBLK)]
ENTRIES = [(0, a, b) for a, b in PAIRS] + [(1, a, b) for a, b in PAIRS if a < b]


def from_partner(block, axis, apart):
    count = lax.axis_size(axis)
    route = []
    for low in range(count):
        high = low | 1 << apart
        if high != low and high < count:
            route += [(low, high), (high, low)]
    return lax.ppermute(block, axis, route)


def spectral_table(freq_bins, block_starts, total_times):
    moments = jnp.arange(total_times)
    offset = moments[None, :] - block_starts[:, None]
    inside = (offset >= 0) & (offset < BLOCK)
    position = offset.astype(jnp.float32)
    taper = 0.5 - 0.5 * jnp.cos(2.0 * math.pi * position / BLOCK)
    turns = jnp.mod(freq_bins[:, None, None] * offset[None, :, :], BLOCK).astype(jnp.float32)
    phase = 2.0 * math.pi * turns / BLOCK
    scaled = jnp.where(inside, taper, 0.0)[None] / math.sqrt(0.375 * BLOCK)
    table = jnp.stack([scaled * jnp.cos(phase), -scaled * jnp.sin(phase)], axis=1)
    return table.reshape(-1, total_times)


def spectra(snap_rows, weights, table):
    fluct = snap_rows - jnp.mean(snap_rows, axis=0, keepdims=True)
    coeffs = jnp.dot(
        table, fluct, precision=lax.Precision.HIGHEST, preferred_element_type=jnp.float32
    )
    return coeffs * jnp.sqrt(weights)[None, :]


def gram_local(coeffs, count):
    vectors = coeffs.reshape(coeffs.shape[0], 2 * coeffs.shape[2], -1)
    return jnp.einsum("fas,fbs->fab", vectors, vectors, precision=lax.Precision.HIGHEST) / count


def gram_split(moment):
    half = moment.shape[-1] // 2
    real_part = moment[:, :half, :half] + moment[:, half:, half:]
    imag_part = moment[:, :half, half:] - moment[:, half:, :half]
    return (real_part, imag_part)


def factor_pair(gram_real, gram_imag):
    order = gram_real.shape[-1]
    columns = jnp.arange(order)
    rows_real = []
    rows_imag = []
    for pivot_row in range(order):
        left_real = gram_real[:, pivot_row, :]
        left_imag = gram_imag[:, pivot_row, :]
        for earlier in range(pivot_row):
            coef_real = rows_real[earlier][:, pivot_row : pivot_row + 1]
            coef_imag = rows_imag[earlier][:, pivot_row : pivot_row + 1]
            left_real = left_real - (
                coef_real * rows_real[earlier] + coef_imag * rows_imag[earlier]
            )
            left_imag = left_imag - (
                coef_real * rows_imag[earlier] - coef_imag * rows_real[earlier]
            )
        pivot = jnp.sqrt(left_real[:, pivot_row : pivot_row + 1])
        rows_real.append(jnp.where(columns >= pivot_row, left_real / pivot, 0.0))
        rows_imag.append(jnp.where(columns > pivot_row, left_imag / pivot, 0.0))
    return (jnp.stack(rows_real, 1), jnp.stack(rows_imag, 1))


def invert_pair(fac_real, fac_imag):
    order = fac_real.shape[-1]
    identity = jnp.eye(order, dtype=fac_real.dtype)
    inv_real = [None] * order
    inv_imag = [None] * order
    for target in reversed(range(order)):
        acc_real = jnp.broadcast_to(identity[target], fac_real[:, 0, :].shape)
        acc_imag = jnp.zeros_like(acc_real)
        for later in range(target + 1, order):
            coef_real = fac_real[:, target, later : later + 1]
            coef_imag = fac_imag[:, target, later : later + 1]
            acc_real = acc_real - (coef_real * inv_real[later] - coef_imag * inv_imag[later])
            acc_imag = acc_imag - (coef_real * inv_imag[later] + coef_imag * inv_real[later])
        diagonal = fac_real[:, target, target : target + 1]
        inv_real[target] = acc_real / diagonal
        inv_imag[target] = acc_imag / diagonal
    return (jnp.stack(inv_real, 1), jnp.stack(inv_imag, 1))


def project(coeffs, inv_real, inv_imag):
    upper = jnp.stack([inv_real, inv_imag], 2)
    lower = jnp.stack([-inv_imag, inv_real], 2)
    kernel = jnp.stack([upper, lower], 1)
    flat = coeffs.reshape(coeffs.shape[0], 2, coeffs.shape[2], -1)
    result = jnp.einsum("fpacb,fpas->fcbs", kernel, flat, precision=lax.Precision.HIGHEST)
    return result.reshape(coeffs.shape)


def any_bands(snapshots, quad_weights, freq_bins, block_starts):
    total_times, local_slabs, slab_cells = snapshots.shape
    table = spectral_table(freq_bins, block_starts, total_times)
    coeffs = spectra(snapshots.reshape(total_times, -1), quad_weights.reshape(-1), table)
    coeffs = coeffs.reshape(NFREQ, 2, NBLK, local_slabs, slab_cells)
    count = SLABS * slab_cells * lax.axis_size("space")
    grouped = lax.all_to_all(coeffs, "band", split_axis=0, concat_axis=3, tiled=True)
    moment = gram_local(grouped, count)
    for level in range(lax.axis_size("space").bit_length() - 1):
        moment = moment + from_partner(moment, "space", level)
    fac_real, fac_imag = factor_pair(*gram_split(moment))
    modes = project(grouped, *invert_pair(fac_real, fac_imag))
    factor = jnp.stack([fac_real, fac_imag], 1)
    return (factor, modes)


def reach(total_times):
    last = total_times - BLOCK
    spans = []
    for j in range(NBLK):
        low = max(GAP_LOW * j, last - GAP_HIGH * (NBLK - 1 - j))
        high = min(GAP_HIGH * j, last - GAP_LOW * (NBLK - 1 - j))
        spans.append((low, high + BLOCK))
    return spans


def fill_table(freq_ref, start_ref, high_ref, low_ref):
    band = lax.axis_index("band")
    wide = BLOCK + LANES
    row = lax.broadcasted_iota(jnp.int32, (NFREQ, wide), 0)
    spot = lax.broadcasted_iota(jnp.int32, (NFREQ, wide), 1)
    bins = jnp.zeros((NFREQ, wide), jnp.int32)
    half = NFREQ // 2
    for r in range(NFREQ):
        owner = 1 - band if r < half else band
        bins = jnp.where(row == r, freq_ref[owner * half + r % half], bins)
    step = 2.0 * math.pi / BLOCK
    phase = ((bins * spot) & (BLOCK - 1)).astype(jnp.float32) * step
    taper = 0.5 - 0.5 * jnp.cos(spot.astype(jnp.float32) * step)
    scaled = jnp.where(spot < BLOCK, taper, 0.0) * (1.0 / math.sqrt(0.375 * BLOCK))
    parts = (scaled * jnp.cos(phase), -scaled * jnp.sin(phase))
    high_ref[...] = jnp.zeros_like(high_ref)
    low_ref[...] = jnp.zeros_like(low_ref)
    for j in range(NBLK):
        start = start_ref[j]
        shift = start % LANES
        place = pl.ds(pl.multiple_of(start - shift, LANES), wide)
        for p in range(2):
            moved = pltpu.roll(parts[p], shift, 1)
            high = moved.astype(jnp.bfloat16)
            low = (moved - high.astype(jnp.float32)).astype(jnp.bfloat16)
            rows = pl.ds((2 * j + p) * NFREQ, NFREQ)
            high_ref[rows, place] = high
            low_ref[rows, place] = low
    return [jnp.sum(part, axis=1, keepdims=True) for part in parts]


def coeff_chunk(flow_ref, total, high_ref, low_ref, fh_ref, fl_ref, acc_ref, low, high, beside):
    apart = flow_ref.shape[0] // total
    per_block = 2 * NFREQ
    spans = reach(total)
    started = [False] * NBLK
    slabs, wide = high - low, (high - low) * LANES
    shift, left = [None] * slabs, [0.0] * slabs
    for i, t0 in enumerate(range(0, total, BLOCK)):
        t1 = min(t0 + BLOCK, total)
        for l in range(slabs):
            values = flow_ref[pl.ds(t0 * apart + low + l, t1 - t0, stride=apart), :]
            if i == 0:
                shift[l] = jnp.sum(values, axis=0, keepdims=True) * (1.0 / (t1 - t0))
            values = values - shift[l]
            left[l] += jnp.sum(values.reshape(-1, ROWS, LANES), axis=0)
            upper = values.astype(jnp.bfloat16)
            cols = slice(l * LANES, (l + 1) * LANES)
            fh_ref[t0:t1, cols] = upper
            fl_ref[t0:t1, cols] = (values - upper.astype(jnp.float32)).astype(jnp.bfloat16)
    for i, t0 in enumerate(range(0, total, BLOCK)):
        t1 = min(t0 + BLOCK, total)
        hit = [j for j in range(NBLK) if spans[j][0] < t1 and spans[j][1] > t0]
        j0, j1 = min(hit), max(hit) + 1
        rows = slice(j0 * per_block, j1 * per_block)
        xh, xl = fh_ref[t0:t1, :wide], fl_ref[t0:t1, :wide]
        th, tl = high_ref[rows, t0:t1], low_ref[rows, t0:t1]
        part = jnp.dot(
            jnp.concatenate([th, tl, th], axis=1),
            jnp.concatenate([xh, xh, xl], axis=0),
            preferred_element_type=jnp.float32,
        )
        for j in range(j0, j1):
            own = slice(j * per_block, (j + 1) * per_block)
            piece = part[(j - j0) * per_block : (j - j0 + 1) * per_block]
            acc_ref[own, :wide] = acc_ref[own, :wide] + piece if started[j] else piece
            started[j] = True
        if beside:
            beside.pop(0)()
    while beside:
        beside.pop(0)()
    left = [jnp.sum(rest, axis=0, keepdims=True) * (1.0 / total) for rest in left]
    return jnp.concatenate(left, axis=1)


def store_chunk(acc_ref, left, sums, root, send_ref, own_ref):
    for p in range(2):
        mean_part = sums[p] * left
        for j in range(NBLK):
            jp = 2 * j + p
            piece = (acc_ref[jp * NFREQ : (jp + 1) * NFREQ, : left.shape[1]] - mean_part) * root
            send_ref[jp] = piece[:ROWS]
            own_ref[jp] = piece[ROWS:]


def spectra_kernel(units, earlier, freq_hbm, start_hbm, weight_hbm, snap_ref, *rest):
    count = len(units)
    total, _, slabs, _ = snap_ref.shape
    send_ref, own_ref, *rest = rest
    if earlier:
        kept_ref, high_ref, low_ref, sums_ref = earlier[1:]
        gram_ref, *rest = rest
    else:
        kept_ref, high_ref, low_ref, sums_ref, *rest = rest
    freq_ref, start_ref, weight_ref, fh_ref, fl_ref, acc_ref, small_sems, held, sems, *rest = rest
    small = [(weight_hbm, weight_ref)]
    if not earlier:
        small += [(freq_hbm, freq_ref), (start_hbm, start_ref)]
    small = [
        pltpu.make_async_copy(source, target, small_sems.at[i])
        for i, (source, target) in enumerate(small)
    ]
    for copy in small:
        copy.start()
    place = count - 1 if not earlier else 0
    targets = [kept_ref if i == place else held.at[i - (i > place)] for i in range(count)]
    copies = [
        pltpu.make_async_copy(snap_ref.at[:, chunk], targets[i], sems.at[i])
        for i, (chunk, _, _) in enumerate(units)
        if i != place or not earlier
    ]
    for copy in copies:
        copy.start()
    for copy in small:
        copy.wait()
    if earlier:
        copies.insert(0, None)
        sums = [sums_ref[p, :, :1] for p in range(2)]
    else:
        sums = fill_table(freq_ref, start_ref, high_ref, low_ref)
        for p in range(2):
            sums_ref[p] = jnp.broadcast_to(sums[p], (NFREQ, LANES))
    beside = gram_steps(earlier[0], slice(None), rest[0], True) if earlier else []
    at = 0
    for i, (chunk, low, high) in enumerate(units):
        weight = weight_ref[:, chunk * LANES : (chunk + 1) * LANES]
        root = jnp.concatenate([jnp.sqrt(weight[l : l + 1, :]) for l in range(low, high)], axis=1)
        if copies[i] is not None:
            copies[i].wait()
        flat = targets[i].reshape(total * slabs, LANES)
        left = coeff_chunk(
            flat, total, high_ref, low_ref, fh_ref, fl_ref, acc_ref, low, high, beside
        )
        cols = slice(at, at + (high - low) * LANES)
        at = cols.stop
        store_chunk(acc_ref, left, sums, root, send_ref.at[:, :, cols], own_ref.at[:, :, cols])
        if earlier:
            beside = gram_steps(send_ref, cols, rest[0], False)
    if earlier:
        for step in beside:
            step()
        gram_ref[...] = fold_lanes([rest[0][e] for e in range(len(ENTRIES))])


def spectra_call(snapshots, weights, freq_bins, block_starts, units, earlier=()):
    total, slabs, cells = snapshots.shape
    by_chunk = snapshots.reshape(total, slabs, -1, LANES).transpose(0, 2, 1, 3)
    cols, count, more = slabs * LANES, len(units), len(earlier)
    values = sum(high - low for _, low, high in units) * LANES
    shapes = [jax.ShapeDtypeStruct((2 * NBLK, ROWS, values), jnp.float32)] * 2
    if more:
        shapes.append(jax.ShapeDtypeStruct((ROWS, LANES), jnp.float32))
    else:
        table = jax.ShapeDtypeStruct((2 * NBLK * NFREQ, total + LANES), jnp.bfloat16)
        shapes.append(jax.ShapeDtypeStruct((total, slabs, LANES), jnp.float32))
        shapes += [table, table, jax.ShapeDtypeStruct((2, NFREQ, LANES), jnp.float32)]
    small = [pltpu.with_memory_space_constraint(v, pltpu.HBM) for v in (freq_bins, block_starts, weights)]
    if not more:
        by_chunk = pltpu.with_memory_space_constraint(by_chunk, pltpu.HBM)
    given = pl.pallas_call(
        lambda *refs: spectra_kernel(units, refs[4 : 4 + more], *refs[:4], *refs[4 + more :]),
        out_shape=tuple(shapes),
        in_specs=[pl.BlockSpec(memory_space=pltpu.HBM)] * 3
        + [pl.BlockSpec(memory_space=pltpu.VMEM if more else pltpu.HBM)]
        + [pl.BlockSpec(memory_space=pltpu.VMEM)] * more,
        out_specs=(pl.BlockSpec(memory_space=pltpu.VMEM),) * len(shapes),
        scratch_shapes=[
            pltpu.SMEM(freq_bins.shape, jnp.int32),
            pltpu.SMEM(block_starts.shape, jnp.int32),
            pltpu.VMEM(weights.shape, jnp.float32),
            pltpu.VMEM((total, cols), jnp.bfloat16),
            pltpu.VMEM((total, cols), jnp.bfloat16),
            pltpu.VMEM((2 * NBLK * NFREQ, cols), jnp.float32),
            pltpu.SemaphoreType.DMA((3,)),
            pltpu.VMEM((count - 1, total, slabs, LANES), jnp.float32),
            pltpu.SemaphoreType.DMA((count,)),
        ]
        + ([pltpu.VMEM((len(ENTRIES), ROWS, LANES), jnp.float32)] if more else []),
        compiler_params=pltpu.CompilerParams(vmem_limit_bytes=VMEM_BYTES),
        cost_estimate=pl.CostEstimate(
            flops=6 * 2 * NBLK * NFREQ * total * values,
            bytes_accessed=4 * (total + 2 * NBLK * NFREQ) * values,
            transcendentals=0,
        ),
        name="spectra",
    )(*small, by_chunk, *earlier)
    return given


def lane_places(count):
    bits = LANES.bit_length() - 1
    used = count.bit_length() - 1
    lanes = []
    for e in range(count):
        lane = 0
        for level in range(used):
            if e >> (used - 1 - level) & 1:
                lane |= 1 << level
        lanes.append(lane)
    return lanes


def fold_lanes(terms):
    lane = lax.broadcasted_iota(jnp.int32, (ROWS, LANES), 1)
    apart = 1
    while len(terms) > 1:
        half = len(terms) // 2
        kept = (lane & apart) == 0
        merged = []
        for i in range(half):
            first, second = terms[i], terms[i + half]
            stay = jnp.where(kept, first, second)
            go = jnp.where(kept, second, first)
            fold = jnp.where(
                kept, pltpu.roll(go, LANES - apart, 1), pltpu.roll(go, apart, 1)
            )
            merged.append(stay + fold)
        terms = merged
        apart *= 2
    total = terms[0]
    while apart < LANES:
        total = total + pltpu.roll(total, apart, 1)
        apart *= 2
    return total


def gram_steps(ref, cols, sums_ref, fresh):
    def step(group):
        start, stop, _ = cols.indices(ref.shape[2])
        keys = [key for key in ENTRIES if key[1] in group]
        totals = [None] * len(keys)
        for k in range(start, stop, LANES):
            re = {b: ref[2 * b, :, k : k + LANES] for b in range(group[0], NBLK)}
            im = {b: ref[2 * b + 1, :, k : k + LANES] for b in range(group[0], NBLK)}
            for i, (kind, a, b) in enumerate(keys):
                if kind == 0:
                    term = re[a] * re[b] + im[a] * im[b]
                else:
                    term = re[a] * im[b] - im[a] * re[b]
                totals[i] = term if totals[i] is None else totals[i] + term
        for key, total in zip(keys, totals):
            e = ENTRIES.index(key)
            sums_ref[e] = total if fresh else sums_ref[e] + total

    return [lambda group=group: step(group) for group in GROUPS]


def gram_kernel(count, *refs):
    out_ref, sums_ref = refs[-2:]
    for i, ref in enumerate(refs[:count]):
        for step in gram_steps(ref, slice(None), sums_ref, i == 0):
            step()
    out_ref[...] = fold_lanes([sums_ref[e] for e in range(len(ENTRIES))])


def gram_call(blocks):
    count = len(blocks)
    return pl.pallas_call(
        lambda *refs: gram_kernel(count, *refs),
        out_shape=jax.ShapeDtypeStruct((ROWS, LANES), jnp.float32),
        in_specs=[pl.BlockSpec(memory_space=pltpu.VMEM)] * count,
        out_specs=pl.BlockSpec(memory_space=pltpu.VMEM),
        scratch_shapes=[pltpu.VMEM((len(ENTRIES), ROWS, LANES), jnp.float32)],
        compiler_params=pltpu.CompilerParams(vmem_limit_bytes=VMEM_BYTES),
        cost_estimate=pl.CostEstimate(
            flops=sum(block.size for block in blocks) * 4 * NBLK,
            bytes_accessed=4 * sum(block.size for block in blocks),
            transcendentals=0,
        ),
        name="gram",
    )(*blocks)


def join_kernel(own_ref, far_ref, _, out_ref):
    out_ref[...] = own_ref[...] + far_ref[...]


def join_call(own, far, after):
    return pl.pallas_call(
        join_kernel,
        out_shape=jax.ShapeDtypeStruct(own.shape, own.dtype),
        in_specs=[pl.BlockSpec(memory_space=pltpu.VMEM)] * 2 + [pl.BlockSpec(memory_space=pl.ANY)],
        out_specs=pl.BlockSpec(memory_space=pltpu.VMEM),
        compiler_params=pltpu.CompilerParams(vmem_limit_bytes=VMEM_BYTES),
        cost_estimate=pl.CostEstimate(flops=JOIN_FLOPS, bytes_accessed=0, transcendentals=0),
        name="join",
    )(own, far, after)


def factor_kernel(count, sum_ref, inv_ref, fac_ref):
    total = sum_ref[...] * (1.0 / count)
    wide = lambda v: jnp.broadcast_to(v, (ROWS, LANES))
    gram = {
        key: wide(total[:, lane : lane + 1]) for key, lane in zip(ENTRIES, lane_places(len(ENTRIES)))
    }
    fac, recip = {}, []
    for r in range(NBLK):
        for c in range(r, NBLK):
            real = gram[0, r, c]
            imag = gram[1, r, c] if c > r else None
            for e in range(r):
                ar, ai = fac[0, e, r], fac[1, e, r]
                br, bi = fac[0, e, c], fac[1, e, c]
                real = real - (ar * br + ai * bi)
                if c > r:
                    imag = imag - (ar * bi - ai * br)
            if c == r:
                pivot = jnp.sqrt(real)
                fac[0, r, r] = pivot
                recip.append(1.0 / pivot)
            else:
                fac[0, r, c] = real * recip[r]
                fac[1, r, c] = imag * recip[r]
    inv = {}
    for b in range(NBLK):
        inv[0, b, b] = recip[b]
        for a in reversed(range(b)):
            real = imag = jnp.zeros((ROWS, LANES), jnp.float32)
            for k in range(a + 1, b + 1):
                cr, ci = fac[0, a, k], fac[1, a, k]
                real = real - cr * inv[0, k, b]
                imag = imag - ci * inv[0, k, b]
                if k < b:
                    real = real + ci * inv[1, k, b]
                    imag = imag - cr * inv[1, k, b]
            inv[0, a, b] = real * recip[a]
            inv[1, a, b] = imag * recip[a]
    for e, key in enumerate(ENTRIES):
        inv_ref[e] = inv[key]
    lane = lax.broadcasted_iota(jnp.int32, (ROWS, LANES), 1)
    for p in range(2):
        for a in range(NBLK):
            line = jnp.zeros((ROWS, LANES), jnp.float32)
            for b in range(a + p, NBLK):
                line = jnp.where(lane == b, fac[p, a, b], line)
            fac_ref[pl.ds(p * NBLK + a, ROWS, stride=2 * NBLK), :] = line


def factor_call(total, count):
    return pl.pallas_call(
        lambda *refs: factor_kernel(count, *refs),
        out_shape=(
            jax.ShapeDtypeStruct((len(ENTRIES), ROWS, LANES), jnp.float32),
            jax.ShapeDtypeStruct((ROWS * 2 * NBLK, LANES), jnp.float32),
        ),
        in_specs=[pl.BlockSpec(memory_space=pltpu.VMEM)],
        out_specs=(pl.BlockSpec(memory_space=pltpu.VMEM),) * 2,
        compiler_params=pltpu.CompilerParams(vmem_limit_bytes=VMEM_BYTES),
        name="factor",
    )(total)


def project_chunk(slabs, inv_ref, spots, flat):
    band = lax.axis_index("band")
    per = flat.shape[0] // ROWS
    for side in range(2):
        base = (band if side == 0 else 1 - band) * slabs
        for l0, (refs, first) in zip(range(0, slabs, 2), spots):
            ref = refs[side]
            cols = [slice(first + i * LANES, first + (i + 1) * LANES) for i in range(2)]
            re = [[ref[2 * a, :, at] for a in range(NBLK)] for at in cols]
            im = [[ref[2 * a + 1, :, at] for a in range(NBLK)] for at in cols]
            for b in range(NBLK):
                diagonal = inv_ref[ENTRIES.index((0, b, b))]
                real = [re[i][b] * diagonal for i in range(2)]
                imag = [im[i][b] * diagonal for i in range(2)]
                for a in range(b):
                    cr = inv_ref[ENTRIES.index((0, a, b))]
                    ci = inv_ref[ENTRIES.index((1, a, b))]
                    for i in range(2):
                        real[i] = real[i] + (re[i][a] * cr - im[i][a] * ci)
                        imag[i] = imag[i] + (re[i][a] * ci + im[i][a] * cr)
                for i in range(2):
                    for p, value in enumerate((real[i], imag[i])):
                        line = (p * NBLK + b) * 2 * slabs + base + l0 + i
                        flat[pl.ds(line, ROWS, stride=per), :] = value


def project_kernel(slabs, pairs, inv_ref, *refs):
    out_ref, held, sems = refs[-3:]
    per = (2 * NBLK + PAD) * 2 * slabs
    copies = []
    for i, places in enumerate(pairs):
        spots = [(refs[2 * which : 2 * which + 2], first) for which, first in places]
        project_chunk(slabs, inv_ref, spots, held.at[i].reshape(ROWS * per, LANES))
        copies.append(
            pltpu.make_async_copy(held.at[i, :, : 2 * NBLK], out_ref.at[:, :, i], sems.at[i])
        )
        copies[i].start()
    for copy in copies:
        copy.wait()


def project_call(inv, arrays, places, slabs):
    count = len(places)
    values = 2 * count * slabs * LANES * ROWS * 2 * NBLK
    return pl.pallas_call(
        lambda *refs: project_kernel(slabs, places, *refs),
        out_shape=jax.ShapeDtypeStruct((ROWS, 2 * NBLK, count, 2 * slabs, LANES), jnp.float32),
        in_specs=[pl.BlockSpec(memory_space=pltpu.VMEM)] * (1 + len(arrays)),
        out_specs=pl.BlockSpec(memory_space=pltpu.HBM),
        scratch_shapes=[
            pltpu.VMEM((count, ROWS, 2 * NBLK + PAD, 2 * slabs, LANES), jnp.float32),
            pltpu.SemaphoreType.DMA((count,)),
        ],
        compiler_params=pltpu.CompilerParams(vmem_limit_bytes=VMEM_BYTES),
        cost_estimate=pl.CostEstimate(
            flops=4 * values * NBLK, bytes_accessed=8 * values, transcendentals=0
        ),
        name="project",
    )(inv, *arrays)


def swap_bands(block):
    return lax.ppermute(block, "band", [(0, 1), (1, 0)])


def two_bands(snapshots, quad_weights, freq_bins, block_starts):
    slabs, cells = snapshots.shape[1:]
    chunks = cells // LANES
    count = 2 * slabs * cells * lax.axis_size("space")
    given = (snapshots, quad_weights, freq_bins, block_starts)
    half = slabs // 2
    early = [(0, 0, slabs), (1, 0, half)]
    late = [(1, half, slabs)] + [(chunk, 0, slabs) for chunk in range(2, chunks)]
    spots = []
    for which, units in enumerate((early, late)):
        pairs = [(chunk, l) for chunk, low, high in units for l in range(low, high, 2)]
        spots += [(place, which, 2 * i * LANES) for i, place in enumerate(pairs)]
    spots = [(which, first) for _, which, first in sorted(spots)]
    spots = [spots[half * chunk : half * (chunk + 1)] for chunk in range(chunks)]
    send_a, own_a, *left = spectra_call(*given, early)
    far_a = swap_bands(send_a)
    send_b, own_b, gram_send = spectra_call(*given, late, [send_a, *left])
    far_gram = swap_bands(gram_send)
    far_b = swap_bands(send_b)
    gram_own = gram_call([own_a, own_b])
    total = join_call(gram_own, far_gram, far_a)
    for level in range(lax.axis_size("space").bit_length() - 1):
        total = total + from_partner(total, "space", level)
    inv, fac = factor_call(total, count)
    modes = project_call(inv, [own_a, far_a, own_b, far_b], spots, slabs)
    modes = modes.reshape(ROWS, 2, NBLK, chunks, 2 * slabs, LANES)
    modes = modes.transpose(0, 1, 2, 4, 3, 5).reshape(ROWS, 2, NBLK, 2 * slabs, cells)
    factor = fac[:, :NBLK].reshape(ROWS, 2, NBLK, NBLK)
    return (factor, modes)


def shards(snapshots, *others):
    fits = NFREQ == ROWS * lax.axis_size("band") == 2 * ROWS
    fits = fits and snapshots.shape[1] == SLABS // 2 and snapshots.shape[2] % LANES == 0
    fits = fits and snapshots.shape[2] > 2 * LANES and snapshots.shape[0] % LANES == 0
    return (two_bands if fits else any_bands)(snapshots, *others)


def solution(mesh):
    placed = (P(None, "band", "space"), P("band", "space"), P(), P())
    return jax.shard_map(
        shards,
        mesh=mesh,
        in_specs=placed,
        out_specs=(P("band", None, None, None), P("band", None, None, None, "space")),
        check_vma=False,
    )
```

```python
import math

import jax
import jax.numpy as jnp
from jax import lax
from jax.experimental import pallas as pl
from jax.experimental.pallas import tpu as pltpu
from jax.sharding import PartitionSpec as P

BLOCK = 256
NBLK = 8
NFREQ = 16
SLABS = 8
GAP_LOW = 64
GAP_HIGH = 192
LANES = 128
ROWS = 8
GROUPS = ((0, 1), (2, 3, 4), (5, 6, 7))
PAD = 1
JOIN_FLOPS = 10**10
VMEM_BYTES = 24 * 1024 * 1024
PAIRS = [(a, b) for a in range(NBLK) for b in range(a, NBLK)]
ENTRIES = [(0, a, b) for a, b in PAIRS] + [(1, a, b) for a, b in PAIRS if a < b]


def from_partner(block, axis, apart):
    count = lax.axis_size(axis)
    route = []
    for low in range(count):
        high = low | 1 << apart
        if high != low and high < count:
            route += [(low, high), (high, low)]
    return lax.ppermute(block, axis, route)


def spectral_table(freq_bins, block_starts, total_times):
    moments = jnp.arange(total_times)
    offset = moments[None, :] - block_starts[:, None]
    inside = (offset >= 0) & (offset < BLOCK)
    position = offset.astype(jnp.float32)
    taper = 0.5 - 0.5 * jnp.cos(2.0 * math.pi * position / BLOCK)
    turns = jnp.mod(freq_bins[:, None, None] * offset[None, :, :], BLOCK).astype(jnp.float32)
    phase = 2.0 * math.pi * turns / BLOCK
    scaled = jnp.where(inside, taper, 0.0)[None] / math.sqrt(0.375 * BLOCK)
    table = jnp.stack([scaled * jnp.cos(phase), -scaled * jnp.sin(phase)], axis=1)
    return table.reshape(-1, total_times)


def spectra(snap_rows, weights, table):
    fluct = snap_rows - jnp.mean(snap_rows, axis=0, keepdims=True)
    coeffs = jnp.dot(
        table, fluct, precision=lax.Precision.HIGHEST, preferred_element_type=jnp.float32
    )
    return coeffs * jnp.sqrt(weights)[None, :]


def gram_local(coeffs, count):
    vectors = coeffs.reshape(coeffs.shape[0], 2 * coeffs.shape[2], -1)
    return jnp.einsum("fas,fbs->fab", vectors, vectors, precision=lax.Precision.HIGHEST) / count


def gram_split(moment):
    half = moment.shape[-1] // 2
    real_part = moment[:, :half, :half] + moment[:, half:, half:]
    imag_part = moment[:, :half, half:] - moment[:, half:, :half]
    return (real_part, imag_part)


def factor_pair(gram_real, gram_imag):
    order = gram_real.shape[-1]
    columns = jnp.arange(order)
    rows_real = []
    rows_imag = []
    for pivot_row in range(order):
        left_real = gram_real[:, pivot_row, :]
        left_imag = gram_imag[:, pivot_row, :]
        for earlier in range(pivot_row):
            coef_real = rows_real[earlier][:, pivot_row : pivot_row + 1]
            coef_imag = rows_imag[earlier][:, pivot_row : pivot_row + 1]
            left_real = left_real - (
                coef_real * rows_real[earlier] + coef_imag * rows_imag[earlier]
            )
            left_imag = left_imag - (
                coef_real * rows_imag[earlier] - coef_imag * rows_real[earlier]
            )
        pivot = jnp.sqrt(left_real[:, pivot_row : pivot_row + 1])
        rows_real.append(jnp.where(columns >= pivot_row, left_real / pivot, 0.0))
        rows_imag.append(jnp.where(columns > pivot_row, left_imag / pivot, 0.0))
    return (jnp.stack(rows_real, 1), jnp.stack(rows_imag, 1))


def invert_pair(fac_real, fac_imag):
    order = fac_real.shape[-1]
    identity = jnp.eye(order, dtype=fac_real.dtype)
    inv_real = [None] * order
    inv_imag = [None] * order
    for target in reversed(range(order)):
        acc_real = jnp.broadcast_to(identity[target], fac_real[:, 0, :].shape)
        acc_imag = jnp.zeros_like(acc_real)
        for later in range(target + 1, order):
            coef_real = fac_real[:, target, later : later + 1]
            coef_imag = fac_imag[:, target, later : later + 1]
            acc_real = acc_real - (coef_real * inv_real[later] - coef_imag * inv_imag[later])
            acc_imag = acc_imag - (coef_real * inv_imag[later] + coef_imag * inv_real[later])
        diagonal = fac_real[:, target, target : target + 1]
        inv_real[target] = acc_real / diagonal
        inv_imag[target] = acc_imag / diagonal
    return (jnp.stack(inv_real, 1), jnp.stack(inv_imag, 1))


def project(coeffs, inv_real, inv_imag):
    upper = jnp.stack([inv_real, inv_imag], 2)
    lower = jnp.stack([-inv_imag, inv_real], 2)
    kernel = jnp.stack([upper, lower], 1)
    flat = coeffs.reshape(coeffs.shape[0], 2, coeffs.shape[2], -1)
    result = jnp.einsum("fpacb,fpas->fcbs", kernel, flat, precision=lax.Precision.HIGHEST)
    return result.reshape(coeffs.shape)


def any_bands(snapshots, quad_weights, freq_bins, block_starts):
    total_times, local_slabs, slab_cells = snapshots.shape
    table = spectral_table(freq_bins, block_starts, total_times)
    coeffs = spectra(snapshots.reshape(total_times, -1), quad_weights.reshape(-1), table)
    coeffs = coeffs.reshape(NFREQ, 2, NBLK, local_slabs, slab_cells)
    count = SLABS * slab_cells * lax.axis_size("space")
    grouped = lax.all_to_all(coeffs, "band", split_axis=0, concat_axis=3, tiled=True)
    moment = gram_local(grouped, count)
    for level in range(lax.axis_size("space").bit_length() - 1):
        moment = moment + from_partner(moment, "space", level)
    fac_real, fac_imag = factor_pair(*gram_split(moment))
    modes = project(grouped, *invert_pair(fac_real, fac_imag))
    factor = jnp.stack([fac_real, fac_imag], 1)
    return (factor, modes)


def reach(total_times):
    last = total_times - BLOCK
    spans = []
    for j in range(NBLK):
        low = max(GAP_LOW * j, last - GAP_HIGH * (NBLK - 1 - j))
        high = min(GAP_HIGH * j, last - GAP_LOW * (NBLK - 1 - j))
        spans.append((low, high + BLOCK))
    return spans


def fill_table(freq_ref, start_ref, high_ref, low_ref):
    band = lax.axis_index("band")
    wide = BLOCK + LANES
    row = lax.broadcasted_iota(jnp.int32, (NFREQ, wide), 0)
    spot = lax.broadcasted_iota(jnp.int32, (NFREQ, wide), 1)
    bins = jnp.zeros((NFREQ, wide), jnp.int32)
    half = NFREQ // 2
    for r in range(NFREQ):
        owner = 1 - band if r < half else band
        bins = jnp.where(row == r, freq_ref[owner * half + r % half], bins)
    step = 2.0 * math.pi / BLOCK
    phase = ((bins * spot) & (BLOCK - 1)).astype(jnp.float32) * step
    taper = 0.5 - 0.5 * jnp.cos(spot.astype(jnp.float32) * step)
    scaled = jnp.where(spot < BLOCK, taper, 0.0) * (1.0 / math.sqrt(0.375 * BLOCK))
    parts = (scaled * jnp.cos(phase), -scaled * jnp.sin(phase))
    high_ref[...] = jnp.zeros_like(high_ref)
    low_ref[...] = jnp.zeros_like(low_ref)
    for j in range(NBLK):
        start = start_ref[j]
        shift = start % LANES
        place = pl.ds(pl.multiple_of(start - shift, LANES), wide)
        for p in range(2):
            moved = pltpu.roll(parts[p], shift, 1)
            high = moved.astype(jnp.bfloat16)
            low = (moved - high.astype(jnp.float32)).astype(jnp.bfloat16)
            rows = pl.ds((2 * j + p) * NFREQ, NFREQ)
            high_ref[rows, place] = high
            low_ref[rows, place] = low
    return [jnp.sum(part, axis=1, keepdims=True) for part in parts]


def coeff_chunk(flow_ref, total, high_ref, low_ref, fh_ref, fl_ref, acc_ref, low, high, beside):
    apart = flow_ref.shape[0] // total
    per_block = 2 * NFREQ
    spans = reach(total)
    started = [False] * NBLK
    slabs, wide = high - low, (high - low) * LANES
    shift, left = [None] * slabs, [0.0] * slabs
    for i, t0 in enumerate(range(0, total, BLOCK)):
        t1 = min(t0 + BLOCK, total)
        for l in range(slabs):
            values = flow_ref[pl.ds(t0 * apart + low + l, t1 - t0, stride=apart), :]
            if i == 0:
                shift[l] = jnp.sum(values, axis=0, keepdims=True) * (1.0 / (t1 - t0))
            values = values - shift[l]
            left[l] += jnp.sum(values.reshape(-1, ROWS, LANES), axis=0)
            upper = values.astype(jnp.bfloat16)
            cols = slice(l * LANES, (l + 1) * LANES)
            fh_ref[t0:t1, cols] = upper
            fl_ref[t0:t1, cols] = (values - upper.astype(jnp.float32)).astype(jnp.bfloat16)
    for i, t0 in enumerate(range(0, total, BLOCK)):
        t1 = min(t0 + BLOCK, total)
        hit = [j for j in range(NBLK) if spans[j][0] < t1 and spans[j][1] > t0]
        j0, j1 = min(hit), max(hit) + 1
        rows = slice(j0 * per_block, j1 * per_block)
        xh, xl = fh_ref[t0:t1, :wide], fl_ref[t0:t1, :wide]
        th, tl = high_ref[rows, t0:t1], low_ref[rows, t0:t1]
        part = jnp.dot(
            jnp.concatenate([th, tl, th], axis=1),
            jnp.concatenate([xh, xh, xl], axis=0),
            preferred_element_type=jnp.float32,
        )
        for j in range(j0, j1):
            own = slice(j * per_block, (j + 1) * per_block)
            piece = part[(j - j0) * per_block : (j - j0 + 1) * per_block]
            acc_ref[own, :wide] = acc_ref[own, :wide] + piece if started[j] else piece
            started[j] = True
        if beside:
            beside.pop(0)()
    while beside:
        beside.pop(0)()
    left = [jnp.sum(rest, axis=0, keepdims=True) * (1.0 / total) for rest in left]
    return jnp.concatenate(left, axis=1)


def store_chunk(acc_ref, left, sums, root, send_ref, own_ref):
    for p in range(2):
        mean_part = sums[p] * left
        for j in range(NBLK):
            jp = 2 * j + p
            piece = (acc_ref[jp * NFREQ : (jp + 1) * NFREQ, : left.shape[1]] - mean_part) * root
            send_ref[jp] = piece[:ROWS]
            own_ref[jp] = piece[ROWS:]


def spectra_kernel(units, earlier, freq_hbm, start_hbm, weight_hbm, snap_ref, *rest):
    count = len(units)
    total, _, slabs, _ = snap_ref.shape
    send_ref, own_ref, *rest = rest
    if earlier:
        kept_ref, high_ref, low_ref, sums_ref = earlier[1:]
        gram_ref, *rest = rest
    else:
        kept_ref, high_ref, low_ref, sums_ref, *rest = rest
    freq_ref, start_ref, weight_ref, fh_ref, fl_ref, acc_ref, small_sems, held, sems, *rest = rest
    small = [(weight_hbm, weight_ref)]
    if not earlier:
        small += [(freq_hbm, freq_ref), (start_hbm, start_ref)]
    small = [
        pltpu.make_async_copy(source, target, small_sems.at[i])
        for i, (source, target) in enumerate(small)
    ]
    for copy in small:
        copy.start()
    place = count - 1 if not earlier else 0
    targets = [kept_ref if i == place else held.at[i - (i > place)] for i in range(count)]
    copies = [
        pltpu.make_async_copy(snap_ref.at[:, chunk], targets[i], sems.at[i])
        for i, (chunk, _, _) in enumerate(units)
        if i != place or not earlier
    ]
    for copy in copies if earlier else copies[:1]:
        copy.start()
    for copy in small:
        copy.wait()
    if earlier:
        copies.insert(0, None)
        sums = [sums_ref[p, :, :1] for p in range(2)]
    else:
        sums = fill_table(freq_ref, start_ref, high_ref, low_ref)
        for p in range(2):
            sums_ref[p] = jnp.broadcast_to(sums[p], (NFREQ, LANES))
        for copy in copies[1:]:
            copy.start()
    beside = gram_steps(earlier[0], slice(None), rest[0], True) if earlier else []
    at = 0
    for i, (chunk, low, high) in enumerate(units):
        weight = weight_ref[:, chunk * LANES : (chunk + 1) * LANES]
        root = jnp.concatenate([jnp.sqrt(weight[l : l + 1, :]) for l in range(low, high)], axis=1)
        if copies[i] is not None:
            copies[i].wait()
        flat = targets[i].reshape(total * slabs, LANES)
        left = coeff_chunk(
            flat, total, high_ref, low_ref, fh_ref, fl_ref, acc_ref, low, high, beside
        )
        cols = slice(at, at + (high - low) * LANES)
        at = cols.stop
        store_chunk(acc_ref, left, sums, root, send_ref.at[:, :, cols], own_ref.at[:, :, cols])
        if earlier:
            beside = gram_steps(send_ref, cols, rest[0], False)
    if earlier:
        for step in beside:
            step()
        gram_ref[...] = fold_lanes([rest[0][e] for e in range(len(ENTRIES))])


def spectra_call(snapshots, weights, freq_bins, block_starts, units, earlier=()):
    total, slabs, cells = snapshots.shape
    by_chunk = snapshots.reshape(total, slabs, -1, LANES).transpose(0, 2, 1, 3)
    cols, count, more = slabs * LANES, len(units), len(earlier)
    values = sum(high - low for _, low, high in units) * LANES
    shapes = [jax.ShapeDtypeStruct((2 * NBLK, ROWS, values), jnp.float32)] * 2
    if more:
        shapes.append(jax.ShapeDtypeStruct((ROWS, LANES), jnp.float32))
    else:
        table = jax.ShapeDtypeStruct((2 * NBLK * NFREQ, total + LANES), jnp.bfloat16)
        shapes.append(jax.ShapeDtypeStruct((total, slabs, LANES), jnp.float32))
        shapes += [table, table, jax.ShapeDtypeStruct((2, NFREQ, LANES), jnp.float32)]
    small = [pltpu.with_memory_space_constraint(v, pltpu.HBM) for v in (freq_bins, block_starts, weights)]
    if not more:
        by_chunk = pltpu.with_memory_space_constraint(by_chunk, pltpu.HBM)
    given = pl.pallas_call(
        lambda *refs: spectra_kernel(units, refs[4 : 4 + more], *refs[:4], *refs[4 + more :]),
        out_shape=tuple(shapes),
        in_specs=[pl.BlockSpec(memory_space=pltpu.HBM)] * 3
        + [pl.BlockSpec(memory_space=pltpu.VMEM if more else pltpu.HBM)]
        + [pl.BlockSpec(memory_space=pltpu.VMEM)] * more,
        out_specs=(pl.BlockSpec(memory_space=pltpu.VMEM),) * len(shapes),
        scratch_shapes=[
            pltpu.SMEM(freq_bins.shape, jnp.int32),
            pltpu.SMEM(block_starts.shape, jnp.int32),
            pltpu.VMEM(weights.shape, jnp.float32),
            pltpu.VMEM((total, cols), jnp.bfloat16),
            pltpu.VMEM((total, cols), jnp.bfloat16),
            pltpu.VMEM((2 * NBLK * NFREQ, cols), jnp.float32),
            pltpu.SemaphoreType.DMA((3,)),
            pltpu.VMEM((count - 1, total, slabs, LANES), jnp.float32),
            pltpu.SemaphoreType.DMA((count,)),
        ]
        + ([pltpu.VMEM((len(ENTRIES), ROWS, LANES), jnp.float32)] if more else []),
        compiler_params=pltpu.CompilerParams(vmem_limit_bytes=VMEM_BYTES),
        cost_estimate=pl.CostEstimate(
            flops=6 * 2 * NBLK * NFREQ * total * values,
            bytes_accessed=4 * (total + 2 * NBLK * NFREQ) * values,
            transcendentals=0,
        ),
        name="spectra",
    )(*small, by_chunk, *earlier)
    return given


def lane_places(count):
    bits = LANES.bit_length() - 1
    used = count.bit_length() - 1
    lanes = []
    for e in range(count):
        lane = 0
        for level in range(used):
            if e >> (used - 1 - level) & 1:
                lane |= 1 << level
        lanes.append(lane)
    return lanes


def fold_lanes(terms):
    lane = lax.broadcasted_iota(jnp.int32, (ROWS, LANES), 1)
    apart = 1
    while len(terms) > 1:
        half = len(terms) // 2
        kept = (lane & apart) == 0
        merged = []
        for i in range(half):
            first, second = terms[i], terms[i + half]
            stay = jnp.where(kept, first, second)
            go = jnp.where(kept, second, first)
            fold = jnp.where(
                kept, pltpu.roll(go, LANES - apart, 1), pltpu.roll(go, apart, 1)
            )
            merged.append(stay + fold)
        terms = merged
        apart *= 2
    total = terms[0]
    while apart < LANES:
        total = total + pltpu.roll(total, apart, 1)
        apart *= 2
    return total


def gram_steps(ref, cols, sums_ref, fresh):
    def step(group):
        start, stop, _ = cols.indices(ref.shape[2])
        keys = [key for key in ENTRIES if key[1] in group]
        totals = [None] * len(keys)
        for k in range(start, stop, LANES):
            re = {b: ref[2 * b, :, k : k + LANES] for b in range(group[0], NBLK)}
            im = {b: ref[2 * b + 1, :, k : k + LANES] for b in range(group[0], NBLK)}
            for i, (kind, a, b) in enumerate(keys):
                if kind == 0:
                    term = re[a] * re[b] + im[a] * im[b]
                else:
                    term = re[a] * im[b] - im[a] * re[b]
                totals[i] = term if totals[i] is None else totals[i] + term
        for key, total in zip(keys, totals):
            e = ENTRIES.index(key)
            sums_ref[e] = total if fresh else sums_ref[e] + total

    return [lambda group=group: step(group) for group in GROUPS]


def gram_kernel(count, *refs):
    out_ref, sums_ref = refs[-2:]
    for i, ref in enumerate(refs[:count]):
        for step in gram_steps(ref, slice(None), sums_ref, i == 0):
            step()
    out_ref[...] = fold_lanes([sums_ref[e] for e in range(len(ENTRIES))])


def gram_call(blocks):
    count = len(blocks)
    return pl.pallas_call(
        lambda *refs: gram_kernel(count, *refs),
        out_shape=jax.ShapeDtypeStruct((ROWS, LANES), jnp.float32),
        in_specs=[pl.BlockSpec(memory_space=pltpu.VMEM)] * count,
        out_specs=pl.BlockSpec(memory_space=pltpu.VMEM),
        scratch_shapes=[pltpu.VMEM((len(ENTRIES), ROWS, LANES), jnp.float32)],
        compiler_params=pltpu.CompilerParams(vmem_limit_bytes=VMEM_BYTES),
        cost_estimate=pl.CostEstimate(
            flops=sum(block.size for block in blocks) * 4 * NBLK,
            bytes_accessed=4 * sum(block.size for block in blocks),
            transcendentals=0,
        ),
        name="gram",
    )(*blocks)


def join_kernel(own_ref, far_ref, _, out_ref):
    out_ref[...] = own_ref[...] + far_ref[...]


def join_call(own, far, after):
    return pl.pallas_call(
        join_kernel,
        out_shape=jax.ShapeDtypeStruct(own.shape, own.dtype),
        in_specs=[pl.BlockSpec(memory_space=pltpu.VMEM)] * 2 + [pl.BlockSpec(memory_space=pl.ANY)],
        out_specs=pl.BlockSpec(memory_space=pltpu.VMEM),
        compiler_params=pltpu.CompilerParams(vmem_limit_bytes=VMEM_BYTES),
        cost_estimate=pl.CostEstimate(flops=JOIN_FLOPS, bytes_accessed=0, transcendentals=0),
        name="join",
    )(own, far, after)


def factor_kernel(count, sum_ref, inv_ref, fac_ref):
    total = sum_ref[...] * (1.0 / count)
    wide = lambda v: jnp.broadcast_to(v, (ROWS, LANES))
    gram = {
        key: wide(total[:, lane : lane + 1]) for key, lane in zip(ENTRIES, lane_places(len(ENTRIES)))
    }
    fac, recip = {}, []
    for r in range(NBLK):
        for c in range(r, NBLK):
            real = gram[0, r, c]
            imag = gram[1, r, c] if c > r else None
            for e in range(r):
                ar, ai = fac[0, e, r], fac[1, e, r]
                br, bi = fac[0, e, c], fac[1, e, c]
                real = real - (ar * br + ai * bi)
                if c > r:
                    imag = imag - (ar * bi - ai * br)
            if c == r:
                pivot = jnp.sqrt(real)
                fac[0, r, r] = pivot
                recip.append(1.0 / pivot)
            else:
                fac[0, r, c] = real * recip[r]
                fac[1, r, c] = imag * recip[r]
    inv = {}
    for b in range(NBLK):
        inv[0, b, b] = recip[b]
        for a in reversed(range(b)):
            real = imag = jnp.zeros((ROWS, LANES), jnp.float32)
            for k in range(a + 1, b + 1):
                cr, ci = fac[0, a, k], fac[1, a, k]
                real = real - cr * inv[0, k, b]
                imag = imag - ci * inv[0, k, b]
                if k < b:
                    real = real + ci * inv[1, k, b]
                    imag = imag - cr * inv[1, k, b]
            inv[0, a, b] = real * recip[a]
            inv[1, a, b] = imag * recip[a]
    for e, key in enumerate(ENTRIES):
        inv_ref[e] = inv[key]
    lane = lax.broadcasted_iota(jnp.int32, (ROWS, LANES), 1)
    for p in range(2):
        for a in range(NBLK):
            line = jnp.zeros((ROWS, LANES), jnp.float32)
            for b in range(a + p, NBLK):
                line = jnp.where(lane == b, fac[p, a, b], line)
            fac_ref[pl.ds(p * NBLK + a, ROWS, stride=2 * NBLK), :] = line


def factor_call(total, count):
    return pl.pallas_call(
        lambda *refs: factor_kernel(count, *refs),
        out_shape=(
            jax.ShapeDtypeStruct((len(ENTRIES), ROWS, LANES), jnp.float32),
            jax.ShapeDtypeStruct((ROWS * 2 * NBLK, LANES), jnp.float32),
        ),
        in_specs=[pl.BlockSpec(memory_space=pltpu.VMEM)],
        out_specs=(pl.BlockSpec(memory_space=pltpu.VMEM),) * 2,
        compiler_params=pltpu.CompilerParams(vmem_limit_bytes=VMEM_BYTES),
        name="factor",
    )(total)


def project_chunk(slabs, inv_ref, spots, flat):
    band = lax.axis_index("band")
    per = flat.shape[0] // ROWS
    for side in range(2):
        base = (band if side == 0 else 1 - band) * slabs
        for l0, (refs, first) in zip(range(0, slabs, 2), spots):
            ref = refs[side]
            cols = [slice(first + i * LANES, first + (i + 1) * LANES) for i in range(2)]
            re = [[ref[2 * a, :, at] for a in range(NBLK)] for at in cols]
            im = [[ref[2 * a + 1, :, at] for a in range(NBLK)] for at in cols]
            for b in range(NBLK):
                diagonal = inv_ref[ENTRIES.index((0, b, b))]
                real = [re[i][b] * diagonal for i in range(2)]
                imag = [im[i][b] * diagonal for i in range(2)]
                for a in range(b):
                    cr = inv_ref[ENTRIES.index((0, a, b))]
                    ci = inv_ref[ENTRIES.index((1, a, b))]
                    for i in range(2):
                        real[i] = real[i] + (re[i][a] * cr - im[i][a] * ci)
                        imag[i] = imag[i] + (re[i][a] * ci + im[i][a] * cr)
                for i in range(2):
                    for p, value in enumerate((real[i], imag[i])):
                        line = (p * NBLK + b) * 2 * slabs + base + l0 + i
                        flat[pl.ds(line, ROWS, stride=per), :] = value


def project_kernel(slabs, pairs, inv_ref, *refs):
    out_ref, held, sems = refs[-3:]
    per = (2 * NBLK + PAD) * 2 * slabs
    copies = []
    for i, places in enumerate(pairs):
        spots = [(refs[2 * which : 2 * which + 2], first) for which, first in places]
        project_chunk(slabs, inv_ref, spots, held.at[i].reshape(ROWS * per, LANES))
        copies.append(
            pltpu.make_async_copy(held.at[i, :, : 2 * NBLK], out_ref.at[:, :, i], sems.at[i])
        )
        copies[i].start()
    for copy in copies:
        copy.wait()


def project_call(inv, arrays, places, slabs):
    count = len(places)
    values = 2 * count * slabs * LANES * ROWS * 2 * NBLK
    return pl.pallas_call(
        lambda *refs: project_kernel(slabs, places, *refs),
        out_shape=jax.ShapeDtypeStruct((ROWS, 2 * NBLK, count, 2 * slabs, LANES), jnp.float32),
        in_specs=[pl.BlockSpec(memory_space=pltpu.VMEM)] * (1 + len(arrays)),
        out_specs=pl.BlockSpec(memory_space=pltpu.HBM),
        scratch_shapes=[
            pltpu.VMEM((count, ROWS, 2 * NBLK + PAD, 2 * slabs, LANES), jnp.float32),
            pltpu.SemaphoreType.DMA((count,)),
        ],
        compiler_params=pltpu.CompilerParams(vmem_limit_bytes=VMEM_BYTES),
        cost_estimate=pl.CostEstimate(
            flops=4 * values * NBLK, bytes_accessed=8 * values, transcendentals=0
        ),
        name="project",
    )(inv, *arrays)


def swap_bands(block):
    return lax.ppermute(block, "band", [(0, 1), (1, 0)])


def two_bands(snapshots, quad_weights, freq_bins, block_starts):
    slabs, cells = snapshots.shape[1:]
    chunks = cells // LANES
    count = 2 * slabs * cells * lax.axis_size("space")
    given = (snapshots, quad_weights, freq_bins, block_starts)
    half = slabs // 2
    early = [(0, 0, slabs), (1, 0, half)]
    late = [(1, half, slabs)] + [(chunk, 0, slabs) for chunk in range(2, chunks)]
    spots = []
    for which, units in enumerate((early, late)):
        pairs = [(chunk, l) for chunk, low, high in units for l in range(low, high, 2)]
        spots += [(place, which, 2 * i * LANES) for i, place in enumerate(pairs)]
    spots = [(which, first) for _, which, first in sorted(spots)]
    spots = [spots[half * chunk : half * (chunk + 1)] for chunk in range(chunks)]
    send_a, own_a, *left = spectra_call(*given, early)
    far_a = swap_bands(send_a)
    send_b, own_b, gram_send = spectra_call(*given, late, [send_a, *left])
    far_gram = swap_bands(gram_send)
    far_b = swap_bands(send_b)
    gram_own = gram_call([own_a, own_b])
    total = join_call(gram_own, far_gram, far_a)
    for level in range(lax.axis_size("space").bit_length() - 1):
        total = total + from_partner(total, "space", level)
    inv, fac = factor_call(total, count)
    modes = project_call(inv, [own_a, far_a, own_b, far_b], spots, slabs)
    modes = modes.reshape(ROWS, 2, NBLK, chunks, 2 * slabs, LANES)
    modes = modes.transpose(0, 1, 2, 4, 3, 5).reshape(ROWS, 2, NBLK, 2 * slabs, cells)
    factor = fac[:, :NBLK].reshape(ROWS, 2, NBLK, NBLK)
    return (factor, modes)


def shards(snapshots, *others):
    fits = NFREQ == ROWS * lax.axis_size("band") == 2 * ROWS
    fits = fits and snapshots.shape[1] == SLABS // 2 and snapshots.shape[2] % LANES == 0
    fits = fits and snapshots.shape[2] > 2 * LANES and snapshots.shape[0] % LANES == 0
    return (two_bands if fits else any_bands)(snapshots, *others)


def solution(mesh):
    placed = (P(None, "band", "space"), P("band", "space"), P(), P())
    return jax.shard_map(
        shards,
        mesh=mesh,
        in_specs=placed,
        out_specs=(P("band", None, None, None), P("band", None, None, None, "space")),
        check_vma=False,
    )
```
